768 devices in a mesh: comp: 8 (over y), tile: 96 (over x, z, core).
Axes of the slice: x: 4, y: 8, z: 12, core: 2. Of those that a mesh axis runs over, the one named last changes fastest.
Arguments:
- atm_flux: bfloat16 [8, 96, 8, 1024], P('comp', 'tile'), may hold values from -6 to 6
- intersection_weight: bfloat16 [8, 96, 8, 12, 128, 128], P('comp', 'tile'), may hold values from 0 to 0.099609375
- src_block: int32 [8, 96, 8, 12], P('comp', 'tile'), may hold values from 0 to 7
- dst_block: int32 [8, 96, 8, 12], P('comp', 'tile'), may hold values from 0 to 7
- intersection_count: int32 [8, 96, 8, 12], P('comp', 'tile'), may hold values from 0 to 128, as said below
- temp: float32 [8, 96, 48, 1024], P('comp', 'tile'), may hold values from -6 to 6
- kappa: float32 [8, 96, 47, 1024], P('comp', 'tile'), may hold values from 0.02 to 0.3
- ssh: float32 [8, 96, 1024], P('comp', 'tile'), may hold values from -6 to 6
- nbr_offset: int32 [8, 96, 6, 1024], P('comp', 'tile'), may hold values from -64 to 64, as said below
- coupler_perm: int32 [8, 96, 1024], P('comp', 'tile'), may hold values from 0 to 1023, each once within a row
Outputs:
- temp_mixed: float32 [8, 96, 48, 1024], P('comp', 'tile')
- ssh_final: float32 [8, 96, 1024], P('comp', 'tile')
- coupler_state: float32 [8, 96, 3, 1024], P('comp', 'tile')
The draws below stay inside these ranges and needn't reach their ends.
Inputs may be any that keep to these rules, and one draw needn't show every extreme that they name: `src_block`: an atmosphere block of the sending device. `dst_block`: an ocean block of the receiving device; some blocks take many slots. `intersection_count`: 0 marks an empty slot; every device has a slot that uses all rows. `nbr_offset`: never 0; both ends are reached on every device. `coupler_perm`: a permutation of each device's cells.
All inputs are finite; a program needn't handle non-finite values.
Results may differ from the reference program's by a relative error of at most 0.00085.
Values sent between devices are 32-bit elements; how exact they have to be, the bound alone decides.
No kernel may reach another device: no remote copies, remote signals or barrier semaphores. Data moves between devices by JAX's collectives and lax.ppermute only.
A program may use at most 32 MiB of HBM per device.

```python
import math
import jax
import jax.numpy as jnp
import numpy as np
from jax import lax

NF = 8
LEV = 48
OC = 1024
AC = 1024
BA = 128
BO = 128
CAP = 12
W = 64
SUB = 8
MIX = 4
N_COMP = 8
N_TILE = 96


def draw_intersection_count(key, part):
    key = jax.random.fold_in(key, 11)
    live_key, size_key = jax.random.split(key)
    shape = (N_COMP, N_TILE, N_COMP, CAP)
    live = (jax.random.randint(live_key, shape, 0, 5) < 3).astype(jnp.int32)
    sizes = jax.random.randint(size_key, shape, 1, BA + 1)
    counts = sizes * live
    return counts.at[:, :, 0, 0].set(BA).astype(jnp.int32)


def draw_nbr_offset(key, part):
    key = jax.random.fold_in(key, 23)
    size_key, sign_key = jax.random.split(key)
    shape = (N_COMP, N_TILE, 6, OC)
    reach = jax.random.randint(size_key, shape, 1, W + 1)
    sign = jax.random.randint(sign_key, shape, 0, 2) * 2 - 1
    offsets = reach * sign
    offsets = offsets.at[:, :, 0, 0].set(W)
    offsets = offsets.at[:, :, 1, 0].set(-W)
    return offsets.astype(jnp.int32)


def plant(array, rng, smallest, top_value):
    extent = array.shape
    index_at = [jax.random.randint(jax.random.fold_in(rng, axis), (), 0, extent[axis]) for axis in range(len(extent))]
    array = array.at[tuple(index_at)].set(smallest)
    longest = extent.index(max(extent))
    index_at[longest] = (index_at[longest] + 1) % extent[longest]
    return array.at[tuple(index_at)].set(top_value)


def level_of(key, dims, cuts, smallest, top_value):
    level, own = 1.0, jax.random.fold_in(key, 6)
    for position, blocks in cuts:
        draws = jnp.exp(jax.random.uniform(jax.random.fold_in(own, position), (blocks,), jnp.float32, smallest / len(cuts), top_value / len(cuts)))
        level = level * jnp.repeat(draws, dims[position] // blocks).reshape([-1 if axis == position else 1 for axis in range(len(dims))])
    return level


def cumulative_ranks(number_of, skew):
    loads = [(1 << 20) // math.isqrt(rank ** skew) + 1 for rank in range(1, number_of + 1)]
    width = 1 + sum(loads) // (1 << 30)
    return np.cumsum(np.array([max(1, weight // width) for weight in loads]))


def skewed_ids(key, shape, amount, slope):
    table = cumulative_ranks(amount, slope)
    ticket = jax.random.randint(jax.random.fold_in(key, 1), shape, 0, int(table[amount - 1]))
    rank = jnp.searchsorted(jnp.asarray(table, jnp.int32), ticket, side="right")
    return jax.random.permutation(jax.random.fold_in(key, 2), amount)[rank].astype(jnp.int32)


def bell_draw(rng, dims, scale, most, shards=(), kind=jnp.bfloat16):
    values = scale * jax.random.normal(rng, dims, jnp.float32)
    if shards:
        values = values * level_of(rng, dims, shards, -0.22, 0.18)
    return jnp.clip(values, -most, most).astype(kind)


def setup_inputs(seed: int = 0) -> dict:
    key_of = jax.random.split(jax.random.key(seed), 11)
    return {
        "atm_flux": bell_draw(key_of[0], (N_COMP, N_TILE, NF, AC), 1.0, 6.0, ((0, 8), (1, 96))),
        "intersection_weight": jnp.clip(0.099609375 * jax.random.uniform(key_of[1], (N_COMP, N_TILE, N_COMP, CAP, BA, BO), jnp.float32) ** level_of(key_of[1], (N_COMP, N_TILE, N_COMP, CAP, BA, BO), ((0, 8), (1, 96)), -0.2, 0.2), 0.0, 0.099609375).astype(jnp.bfloat16),
        "src_block": plant(jax.random.randint(key_of[2], (N_COMP, N_TILE, N_COMP, CAP), 0, AC // BA), jax.random.fold_in(key_of[2], 1), 0, (AC // BA) - 1).astype(jnp.int32),
        "dst_block": plant(skewed_ids(key_of[3], (N_COMP, N_TILE, N_COMP, CAP), OC // BO, 2), jax.random.fold_in(key_of[3], 3), 0, (OC // BO) - 1).astype(jnp.int32),
        "intersection_count": draw_intersection_count(jax.random.fold_in(key_of[10], 71), 0),
        "temp": bell_draw(key_of[5], (N_COMP, N_TILE, LEV, OC), 1.0, 6.0, ((0, 8), (1, 96)), jnp.float32),
        "kappa": jnp.clip(0.02 + 0.28 * jax.random.uniform(key_of[6], (N_COMP, N_TILE, LEV - 1, OC), jnp.float32) ** level_of(key_of[6], (N_COMP, N_TILE, LEV - 1, OC), ((0, 8), (1, 96)), -0.2, 0.2), 0.02, 0.3),
        "ssh": bell_draw(key_of[7], (N_COMP, N_TILE, OC), 1.0, 6.0, ((0, 8), (1, 96)), jnp.float32),
        "nbr_offset": draw_nbr_offset(jax.random.fold_in(key_of[10], 71), 0),
        "coupler_perm": jax.vmap(lambda own: jax.random.permutation(own, OC))(jax.random.split(key_of[9], N_COMP * N_TILE)).reshape((N_COMP, N_TILE, OC)).astype(jnp.int32),
    }


heat_gain = 0.5
shortwave_gain = 0.5
wind_mixing = 0.15
relax_rate = 0.5
fresh_gain = 0.5

def slot_terms(flux_dev, weight_dev, source_dev, count_dev):
    blocks = flux_dev.reshape(NF, AC // BA, BA).transpose(1, 0, 2)
    picked = blocks[source_dev.reshape(-1)]
    rows = jnp.arange(BA, dtype=jnp.int32)
    keep = (rows[None, :] < count_dev.reshape(-1)[:, None]).astype(picked.dtype)
    picked = picked * keep[:, None, :]
    terms = jnp.einsum('mnr,mro->mno', picked.astype(jnp.float32), weight_dev.reshape(-1, BA, BO).astype(jnp.float32))
    return terms.reshape(N_COMP, CAP, NF, BO)

def column_update(temp, kappa, forcing):
    levels = jnp.arange(LEV).astype(jnp.float32)
    shallow = jnp.exp(-levels / 4.0) - jnp.exp(-(levels + 1.0) / 4.0)
    heated = temp + shortwave_gain * forcing[..., 1:2, :] * shallow[:, None]
    top = heat_gain * (forcing[..., 0, :] + forcing[..., 7, :])
    heated = heated.at[..., 0, :].add(top)
    wind = jnp.sqrt(forcing[..., 2, :] * forcing[..., 2, :] + forcing[..., 3, :] * forcing[..., 3, :])
    decay = jnp.exp(-levels[:LEV - 1] / 4.0)
    keff = kappa + wind_mixing * jnp.tanh(wind)[..., None, :] * decay[:, None]
    for sweep in range(MIX):
        flow = keff * (heated[..., 1:, :] - heated[..., :-1, :])
        zero = jnp.zeros_like(flow[..., :1, :])
        heated = heated + jnp.concatenate([flow, zero], axis=-2) - jnp.concatenate([zero, flow], axis=-2)
    return heated

def reference(atm_flux, intersection_weight, src_block, dst_block, intersection_count, temp, kappa, ssh, nbr_offset, coupler_perm):
    devices = N_COMP * N_TILE
    flat_flux = atm_flux.reshape(devices, NF, AC)
    flat_weight = intersection_weight.reshape(devices, N_COMP, CAP, BA, BO)
    flat_source = src_block.reshape(devices, N_COMP, CAP)
    flat_count = intersection_count.reshape(devices, N_COMP, CAP)
    terms = lax.map(lambda items: slot_terms(*items), (flat_flux, flat_weight, flat_source, flat_count))
    terms = terms.reshape(N_COMP, N_TILE, N_COMP, CAP, NF, BO)
    blocks_out = OC // BO
    onehot = (dst_block[..., None] == jnp.arange(blocks_out, dtype=jnp.int32)).astype(jnp.float32)
    forcing = jnp.einsum('dtckb,ctdkno->dtbno', onehot, terms, precision=lax.Precision.HIGHEST)
    forcing = forcing.transpose(0, 1, 3, 2, 4).reshape(N_COMP, N_TILE, NF, OC)
    temp_mixed = column_update(temp, kappa, forcing)
    total = N_TILE * OC
    band = ssh.reshape(N_COMP, total)
    offsets = nbr_offset.transpose(0, 2, 1, 3).reshape(N_COMP, 6, total)
    places = (jnp.arange(total, dtype=jnp.int32)[None, None, :] + offsets) % total
    fresh = (forcing[:, :, 5] - forcing[:, :, 4] + forcing[:, :, 6]).reshape(N_COMP, total)
    for step in range(SUB):
        spread = jnp.broadcast_to(band[:, None, :], (N_COMP, 6, total))
        near = jnp.take_along_axis(spread, places, axis=2)
        average = lax.optimization_barrier(jnp.sum(near, axis=1)) / 6.0
        band = band + relax_rate * (average - band) + fresh_gain * fresh / SUB
    ssh_final = band.reshape(N_COMP, N_TILE, OC)
    state = jnp.stack([temp_mixed[:, :, 0], temp_mixed[:, :, 1], ssh_final], axis=2)
    order = jnp.broadcast_to(coupler_perm[:, :, None, :], (N_COMP, N_TILE, 3, OC))
    permuted = jnp.take_along_axis(state, order, axis=3)
    share = OC // N_COMP
    permuted = permuted.reshape(N_COMP, N_TILE, 3, N_COMP, share)
    coupler_state = permuted.transpose(3, 1, 2, 0, 4).reshape(N_COMP, N_TILE, 3, OC)
    return (temp_mixed, ssh_final, coupler_state)
```

```python
import jax
import jax.numpy as jnp
from jax import lax
from jax.experimental import pallas as pl
from jax.experimental.pallas import tpu as pltpu
from jax.sharding import PartitionSpec as P

SUB = 8
MIX = 4
LANES = 128
FIELDS = 5

heat_gain = 0.5
shortwave_gain = 0.5
wind_mixing = 0.15
relax_rate = 0.5
fresh_gain = 0.5


def shape_of(dims, dtype=jnp.float32):
    return jax.ShapeDtypeStruct(dims, dtype)


def terms_kernel(src_ref, cnt_ref, flux_ref, weight_ref, out_ref, blocks_ref, term_ref):
    d = pl.program_id(0)
    slots = weight_ref.shape[1]
    nb = blocks_ref.shape[0]

    @pl.when(d == 0)
    def _():
        for b in range(nb):
            blocks_ref[b] = flux_ref[:, b * LANES : (b + 1) * LANES].astype(jnp.float32)

    lane = lax.broadcasted_iota(jnp.int32, (8, LANES), 1)
    zero = jnp.zeros((8, LANES), jnp.float32)
    for k in range(0, slots, 2):
        parts = []
        for i in (0, 1):
            block = blocks_ref[src_ref[0, 0, d, k + i]]
            parts.append(jnp.where(lane < cnt_ref[0, 0, d, k + i], block, zero))
        top = jnp.concatenate([parts[0], zero], axis=1)
        low = jnp.concatenate([zero, parts[1]], axis=1)
        lhs = jnp.concatenate([top, low], axis=0).astype(jnp.bfloat16)
        rhs = weight_ref[0, k : k + 2].reshape(2 * LANES, LANES)
        term_ref[k * 8 : k * 8 + 16, :] = jnp.dot(lhs, rhs, preferred_element_type=jnp.float32)

    def field(f):
        return term_ref[pl.ds(f, slots, stride=8), :]

    out_ref[0, 0:slots] = field(1)
    out_ref[0, slots : 2 * slots] = field(0) + field(7)
    out_ref[0, 2 * slots : 3 * slots] = field(2)
    out_ref[0, 3 * slots : 4 * slots] = field(3)
    out_ref[0, 4 * slots : 5 * slots] = field(5) - field(4) + field(6)
    rest = out_ref.shape[1] - FIELDS * slots
    if rest:
        out_ref[0, FIELDS * slots :] = jnp.zeros((rest, LANES), jnp.float32)


def remap_terms(src, cnt, flux, weights):
    groups, slots = weights.shape[:2]
    rows = -(-FIELDS * slots // 8) * 8
    smem = pl.BlockSpec(memory_space=pltpu.SMEM)
    return pl.pallas_call(
        terms_kernel,
        grid=(groups,),
        in_specs=[
            smem,
            smem,
            pl.BlockSpec(flux.shape, lambda d: (0, 0)),
            pl.BlockSpec((1,) + weights.shape[1:], lambda d: (d, 0, 0, 0)),
        ],
        out_specs=pl.BlockSpec((1, rows, LANES), lambda d: (d, 0, 0)),
        out_shape=shape_of((groups, rows, LANES)),
        scratch_shapes=[
            pltpu.VMEM((flux.shape[1] // LANES, 8, LANES), jnp.float32),
            pltpu.VMEM((slots * 8, LANES), jnp.float32),
        ],
    )(src, cnt, flux, weights)


def forcing_kernel(odd_ref, arrived_ref, dst_ref, ssh_ref, off_ref, forcing_ref, offs_ref, pay0_ref, pay1_ref):
    groups, rows, _ = arrived_ref.shape
    slots = dst_ref.shape[1]
    dst = dst_ref[...]
    parts = [dst + 8 * f for f in range(FIELDS)]
    rest = rows - FIELDS * slots
    if rest:
        parts.append(jnp.full((groups, rest), -1, jnp.int32))
    ids = jnp.concatenate(parts, axis=1)
    targets = lax.broadcasted_iota(jnp.int32, (FIELDS * 8, rows), 0)
    total = jnp.zeros((FIELDS * 8, LANES), jnp.float32)
    for c in range(groups):
        onehot = (jnp.broadcast_to(ids[c : c + 1, :], targets.shape) == targets).astype(jnp.float32)
        onehot = onehot.astype(jnp.bfloat16)
        rest_of = arrived_ref[c]
        for _ in range(3):
            piece = rest_of.astype(jnp.bfloat16)
            total = total + jnp.dot(onehot, piece, preferred_element_type=jnp.float32)
            rest_of = rest_of - piece.astype(jnp.float32)
    forcing_ref[...] = total
    offsets = off_ref.shape[0]
    for b in range(8):
        cols = off_ref[:, b * LANES : (b + 1) * LANES].astype(jnp.float32)
        offs_ref[pl.ds(b, offsets, stride=8), :] = cols
    odd = odd_ref[0] == 1
    pieces = [ssh_ref[...], total[(FIELDS - 1) * 8 :]]
    pieces += [offs_ref[j * 8 : j * 8 + 8, :] for j in range(offsets)]
    for i, x in enumerate(pieces):
        pay0_ref[4 * i : 4 * i + 4, :] = jnp.where(odd, x[0:4], x[4:8])
        pay1_ref[4 * i : 4 * i + 4, :] = jnp.where(odd, x[4:8], x[0:4])


def forcing_and_halo(odd, arrived, dst, ssh, offsets):
    vmem = pl.BlockSpec(memory_space=pltpu.VMEM)
    count = offsets.shape[0]
    pay = shape_of((4 * (2 + count), LANES))
    return pl.pallas_call(
        forcing_kernel,
        in_specs=[pl.BlockSpec(memory_space=pltpu.SMEM)] + [vmem] * 4,
        out_specs=[vmem] * 4,
        out_shape=[shape_of((FIELDS * 8, LANES)), shape_of((count * 8, LANES)), pay, pay],
    )(odd, arrived, dst, ssh, offsets)


def column_kernel(temp_ref, kappa_ref, forcing_ref, mixed_ref, top_ref):
    levels = temp_ref.shape[0]
    level = lax.broadcasted_iota(jnp.int32, (levels, LANES), 0)
    depth = level.astype(jnp.float32)
    decay = jnp.exp(-depth / 4.0)
    shallow = shortwave_gain * (decay - jnp.exp(-(depth + 1.0) / 4.0))
    decay = jnp.where(level < levels - 1, decay, 0.0)
    east, north = forcing_ref[16:24, :], forcing_ref[24:32, :]
    mixing = wind_mixing * jnp.tanh(jnp.sqrt(east * east + north * north))
    top = heat_gain * forcing_ref[8:16, :]
    short = forcing_ref[0:8, :]
    last = jnp.zeros((1, LANES), jnp.float32)
    for b in range(temp_ref.shape[1] // LANES):
        cols = slice(b * LANES, (b + 1) * LANES)

        def row(x):
            return jnp.broadcast_to(x[b : b + 1, :], (levels, LANES))

        heated = temp_ref[:, cols] + row(short) * shallow
        heated = heated + jnp.where(level == 0, row(top), 0.0)
        keff = jnp.concatenate([kappa_ref[:, cols], last], axis=0) + row(mixing) * decay
        for _ in range(MIX):
            flow = keff * (pltpu.roll(heated, levels - 1, 0) - heated)
            heated = heated + flow - pltpu.roll(flow, 1, 0)
        mixed_ref[:, cols] = heated
        top_ref[b : b + 1, :] = heated[0:1]
        top_ref[8 + b : 9 + b, :] = heated[1:2]


def column_update(temp, kappa, forcing):
    vmem = pl.BlockSpec(memory_space=pltpu.VMEM)
    return pl.pallas_call(
        column_kernel,
        in_specs=[vmem] * 3,
        out_specs=[vmem] * 2,
        out_shape=[shape_of(temp.shape), shape_of((16, LANES))],
        cost_estimate=pl.CostEstimate(
            flops=40 * temp.size, bytes_accessed=12 * temp.size, transcendentals=2048
        ),
    )(temp, kappa, forcing)


def pick(x, idx):
    return jnp.take_along_axis(x, idx, axis=1, mode="promise_in_bounds")


def height_kernel(odd_ref, got0_ref, got1_ref, ssh_ref, fresh_ref, offs_ref, top_ref, perm_ref, ssh_out, state_out):
    odd = odd_ref[0] == 1
    count = offs_ref.shape[0] // 8

    def extended(i, own):
        a, b = got0_ref[4 * i : 4 * i + 4, :], got1_ref[4 * i : 4 * i + 4, :]
        left, right = jnp.where(odd, a, b), jnp.where(odd, b, a)
        return jnp.concatenate([left, own, right], axis=0)

    eta = extended(0, ssh_ref[...])
    fresh = (fresh_gain / SUB) * extended(1, fresh_ref[...])
    lane = lax.broadcasted_iota(jnp.int32, (16, LANES), 1)
    places, crossing = [], []
    for j in range(count):
        target = lane + extended(2 + j, offs_ref[j * 8 : j * 8 + 8, :]).astype(jnp.int32)
        places.append(target & (LANES - 1))
        crossing.append((target < 0) | (target >= LANES))
    upper = lane >= LANES // 2
    for _ in range(SUB):
        beside = jnp.where(upper, pltpu.roll(eta, 1, 0), pltpu.roll(eta, 15, 0))
        halves = []
        for h in (0, 8):
            here, other = eta[h : h + 8], beside[h : h + 8]
            near = None
            for j in range(count):
                idx = places[j][h : h + 8]
                value = jnp.where(crossing[j][h : h + 8], pick(other, idx), pick(here, idx))
                near = value if near is None else near + value
            halves.append(near)
        average = jnp.concatenate(halves, axis=0) / 6.0
        eta = eta + relax_rate * (average - eta) + fresh
    height = eta[4:12]
    ssh_out[...] = height
    perm = perm_ref[...]
    row, col = perm >> 7, perm & (LANES - 1)
    for f, x in enumerate((top_ref[0:8, :], top_ref[8:16, :], height)):
        out = jnp.zeros((8, LANES), jnp.float32)
        for s in range(8):
            out = jnp.where(row == s, pick(jnp.broadcast_to(x[s : s + 1, :], (8, LANES)), col), out)
        for d in range(8):
            state_out[d, f : f + 1, :] = out[d : d + 1]


def heights_and_state(odd, got0, got1, ssh, fresh, offs, top, perm):
    vmem = pl.BlockSpec(memory_space=pltpu.VMEM)
    return pl.pallas_call(
        height_kernel,
        in_specs=[pl.BlockSpec(memory_space=pltpu.SMEM)] + [vmem] * 7,
        out_specs=[vmem] * 2,
        out_shape=[shape_of((8, LANES)), shape_of((8, 3, LANES))],
    )(odd, got0, got1, ssh, fresh, offs, top, perm)


def per_device(
    atm_flux,
    intersection_weight,
    src_block,
    dst_block,
    intersection_count,
    temp,
    kappa,
    ssh,
    nbr_offset,
    coupler_perm,
):
    tiles = lax.axis_size("tile")
    odd = (lax.axis_index("tile") % 2).astype(jnp.int32).reshape(1)
    height = ssh.reshape(8, LANES)
    perm = coupler_perm.reshape(8, LANES)
    terms = remap_terms(src_block, intersection_count, atm_flux[0, 0], intersection_weight[0, 0])
    arrived = lax.all_to_all(terms, "comp", split_axis=0, concat_axis=0, tiled=True)
    forcing, offs, pay0, pay1 = forcing_and_halo(
        odd, arrived, dst_block[0, 0], height, nbr_offset[0, 0]
    )
    inner = [(i, i ^ 1) for i in range(tiles)]
    outer = [(i, (i - 1 if i % 2 == 0 else i + 1) % tiles) for i in range(tiles)]
    got1 = lax.ppermute(pay1, "tile", outer)
    got0 = lax.ppermute(pay0, "tile", inner)
    mixed, top = column_update(temp[0, 0], kappa[0, 0], forcing)
    height, state = heights_and_state(
        odd, got0, got1, height, forcing[(FIELDS - 1) * 8 :], offs, top, perm
    )
    relaid = lax.all_to_all(state, "comp", split_axis=0, concat_axis=0, tiled=True)
    coupler_state = relaid.transpose(1, 0, 2).reshape(1, 1, 3, -1)
    return (mixed[None, None], height.reshape(ssh.shape), coupler_state)


def solution(mesh):
    return jax.shard_map(
        per_device,
        mesh=mesh,
        in_specs=(
            P("comp", "tile", None, None),
            P("comp", "tile", None, None, None, None),
            P("comp", "tile", None, None),
            P("comp", "tile", None, None),
            P("comp", "tile", None, None),
            P("comp", "tile", None, None),
            P("comp", "tile", None, None),
            P("comp", "tile", None),
            P("comp", "tile", None, None),
            P("comp", "tile", None),
        ),
        out_specs=(
            P("comp", "tile", None, None),
            P("comp", "tile", None),
            P("comp", "tile", None, None),
        ),
        check_vma=False,
    )
```

```python
import functools
import math

import jax
import jax.numpy as jnp
from jax import lax
from jax.experimental import pallas as pl
from jax.experimental.pallas import tpu as pltpu
from jax.sharding import PartitionSpec as P

SUB = 8
MIX = 4
LANES = 128
FIELDS = 5

heat_gain = 0.5
shortwave_gain = 0.5
wind_mixing = 0.15
relax_rate = 0.5
fresh_gain = 0.5


def shape_of(dims, dtype=jnp.float32):
    return jax.ShapeDtypeStruct(dims, dtype)


def limit(mib):
    return pltpu.CompilerParams(vmem_limit_bytes=mib << 20)


def cost(flops, moved):
    return pl.CostEstimate(flops=flops, bytes_accessed=moved, transcendentals=0)


VMEM = pl.BlockSpec(memory_space=pltpu.VMEM)
SMEM = pl.BlockSpec(memory_space=pltpu.SMEM)
ANY = pl.BlockSpec(memory_space=pl.ANY)


def terms_kernel(src_ref, cnt_ref, flux_ref, weight_ref, out_ref, blocks_ref, term_ref, held_ref, sems):
    groups, slots = weight_ref.shape[:2]
    copies = [
        pltpu.make_async_copy(weight_ref.at[d], held_ref.at[d], sems.at[d]) for d in range(groups)
    ]
    for copy in copies:
        copy.start()
    for b in range(blocks_ref.shape[0]):
        blocks_ref[b] = flux_ref[:, b * LANES : (b + 1) * LANES].astype(jnp.float32)
    lane = lax.broadcasted_iota(jnp.int32, (8, LANES), 1)
    zero = jnp.zeros((8, LANES), jnp.float32)
    rest = out_ref.shape[1] - FIELDS * slots
    for d in range(groups):
        copies[d].wait()
        for k in range(0, slots, 2):
            parts = []
            for i in (0, 1):
                block = blocks_ref[src_ref[0, 0, d, k + i]]
                parts.append(jnp.where(lane < cnt_ref[0, 0, d, k + i], block, zero))
            top = jnp.concatenate([parts[0], zero], axis=1)
            low = jnp.concatenate([zero, parts[1]], axis=1)
            lhs = jnp.concatenate([top, low], axis=0).astype(jnp.bfloat16)
            rhs = held_ref[d, k : k + 2].reshape(2 * LANES, LANES)
            term_ref[d, k * 8 : k * 8 + 16, :] = jnp.dot(
                lhs, rhs, preferred_element_type=jnp.float32
            )
        f = [term_ref[d, pl.ds(i, slots, stride=8), :] for i in range(8)]
        for i, x in enumerate((f[1], f[0] + f[7], f[2], f[3], f[5] - f[4] + f[6])):
            out_ref[d, i * slots : (i + 1) * slots] = x
        if rest:
            out_ref[d, FIELDS * slots :] = jnp.zeros((rest, LANES), jnp.float32)


def remap_terms(src, cnt, flux, weights):
    groups, slots = weights.shape[:2]
    rows = -(-FIELDS * slots // 8) * 8
    return pl.pallas_call(
        terms_kernel,
        in_specs=[SMEM, SMEM, VMEM, ANY],
        out_specs=VMEM,
        out_shape=shape_of((groups, rows, LANES)),
        scratch_shapes=[
            pltpu.VMEM((flux.shape[1] // LANES, 8, LANES), jnp.float32),
            pltpu.VMEM((groups, slots * 8, LANES), jnp.float32),
            pltpu.VMEM(weights.shape, weights.dtype),
            pltpu.SemaphoreType.DMA((groups,)),
        ],
    )(src, cnt, flux, weights)


def target_kernel(after_ref, dst_ref, out_ref, *, rows):
    groups, slots = dst_ref.shape
    dst = dst_ref[...]
    parts = [dst + 8 * f for f in range(FIELDS)]
    rest = rows - FIELDS * slots
    if rest:
        parts.append(jnp.full((groups, rest), -1, jnp.int32))
    ids = jnp.concatenate(parts, axis=1)
    line = jnp.concatenate([ids[c : c + 1, :] for c in range(groups)], axis=1)
    targets = lax.broadcasted_iota(jnp.int32, out_ref.shape, 0)
    hit = jnp.broadcast_to(line, out_ref.shape) == targets
    out_ref[...] = hit.astype(jnp.float32).astype(jnp.bfloat16)


def one_hot_targets(after, dst):
    groups, rows, _ = after.shape
    return pl.pallas_call(
        functools.partial(target_kernel, rows=rows),
        in_specs=[ANY, VMEM],
        out_specs=VMEM,
        out_shape=shape_of((48, groups * rows), jnp.bfloat16),
        cost_estimate=cost(1 << 20, 1 << 20),
        compiler_params=limit(4),
    )(after, dst)


def forcing_kernel(odd_ref, arrived_ref, onehot_ref, ssh_ref, off_ref, forcing_ref, pay0_ref, pay1_ref):
    onehot = onehot_ref[...]
    rest = arrived_ref[...].reshape(-1, LANES)
    total = None
    for _ in range(3):
        piece = rest.astype(jnp.bfloat16)
        part = jnp.dot(onehot, piece, preferred_element_type=jnp.float32)
        total = part if total is None else total + part
        rest = rest - piece.astype(jnp.float32)
    forcing_ref[...] = total[: FIELDS * 8]
    odd = odd_ref[0] == 1
    pieces = [ssh_ref[...], total[(FIELDS - 1) * 8 : FIELDS * 8]]
    pieces += [off_ref[j].astype(jnp.float32) for j in range(off_ref.shape[0])]
    for i, x in enumerate(pieces):
        pay0_ref[4 * i : 4 * i + 4, :] = jnp.where(odd, x[0:4], x[4:8])
        pay1_ref[4 * i : 4 * i + 4, :] = jnp.where(odd, x[4:8], x[0:4])


def forcing_and_halo(odd, arrived, onehot, ssh, offsets):
    pay = shape_of((4 * (2 + offsets.shape[0]), LANES))
    return pl.pallas_call(
        forcing_kernel,
        in_specs=[SMEM] + [VMEM] * 4,
        out_specs=[VMEM] * 3,
        out_shape=[shape_of((FIELDS * 8, LANES)), pay, pay],
        compiler_params=limit(4),
    )(odd, arrived, onehot, ssh, offsets)


def column_parts(forcing_ref):
    east, north = forcing_ref[16:24, :], forcing_ref[24:32, :]
    mixing = wind_mixing * jnp.tanh(jnp.sqrt(east * east + north * north))
    return shortwave_gain * forcing_ref[0:8, :], heat_gain * forcing_ref[8:16, :], mixing


def mix_levels(kappa_ref, forcing_ref, tile_ref, levels):
    short, top, mixing = column_parts(forcing_ref)
    heated, keff = [], []
    for level in range(levels):
        shallow = math.exp(-level / 4.0) - math.exp(-(level + 1.0) / 4.0)
        value = tile_ref[level * 8 : level * 8 + 8, :] + short * shallow
        heated.append(value + top if level == 0 else value)
        if level < levels - 1:
            keff.append(kappa_ref[level] + mixing * math.exp(-level / 4.0))
    for _ in range(MIX):
        above = None
        for level in range(levels):
            here = heated[level]
            if level < levels - 1:
                below = keff[level] * (heated[level + 1] - here)
                new = here + below
            else:
                new = here
            heated[level] = new if above is None else new - above
            above = below
    return heated


def permuted(x, row, col):
    out = jnp.zeros((8, LANES), jnp.float32)
    for s in range(8):
        out = jnp.where(row == s, pick(jnp.broadcast_to(x[s : s + 1, :], (8, LANES)), col), out)
    return out


def pick(x, idx):
    return jnp.take_along_axis(x, idx, axis=1, mode="promise_in_bounds")


def surface_kernel(temp_ref, kappa_ref, forcing_ref, perm_ref, out_ref, tile_ref):
    for b in range(8):
        tile_ref[pl.ds(b, 8, stride=8), :] = temp_ref[:, b * LANES : (b + 1) * LANES]
    heated = mix_levels(kappa_ref, forcing_ref, tile_ref, MIX + 3)
    perm = perm_ref[...]
    row, col = perm >> 7, perm & (LANES - 1)
    for f in (0, 1):
        out_ref[f] = permuted(heated[f], row, col)


def surface_rows(temp, kappa, forcing, perm):
    return pl.pallas_call(
        surface_kernel,
        grid=(1,),
        in_specs=[
            pl.BlockSpec((8, temp.shape[1]), lambda i: (0, 0)),
            pl.BlockSpec((8, 8, LANES), lambda i: (0, 0, 0)),
            pl.BlockSpec(forcing.shape, lambda i: (0, 0)),
            pl.BlockSpec(perm.shape, lambda i: (0, 0)),
        ],
        out_specs=pl.BlockSpec((2, 8, LANES), lambda i: (0, 0, 0)),
        out_shape=shape_of((2, 8, LANES)),
        scratch_shapes=[pltpu.VMEM((64, LANES), jnp.float32)],
        cost_estimate=cost(1 << 20, 1 << 20),
        compiler_params=limit(4),
    )(temp, kappa, forcing, perm)


def column_kernel(after_ref, temp_ref, kappa_ref, forcing_ref, mixed_ref, tile_ref):
    levels = temp_ref.shape[0]
    for b in range(8):
        tile_ref[pl.ds(b, levels, stride=8), :] = temp_ref[:, b * LANES : (b + 1) * LANES]
    heated = mix_levels(kappa_ref, forcing_ref, tile_ref, levels)
    for level in range(levels):
        tile_ref[level * 8 : level * 8 + 8, :] = heated[level]
    for b in range(8):
        mixed_ref[:, b * LANES : (b + 1) * LANES] = tile_ref[pl.ds(b, levels, stride=8), :]


def column_update(after, temp, kappa, forcing):
    return pl.pallas_call(
        column_kernel,
        in_specs=[ANY] + [VMEM] * 3,
        out_specs=VMEM,
        out_shape=shape_of(temp.shape),
        scratch_shapes=[pltpu.VMEM((temp.shape[0] * 8, LANES), jnp.float32)],
        cost_estimate=cost(1 << 22, 1 << 22),
        compiler_params=limit(4),
    )(after, temp, kappa, forcing)


def height_kernel(odd_ref, got0_ref, got1_ref, ssh_ref, forcing_ref, off_ref, top_ref, perm_ref, ssh_out, state_out):
    odd = odd_ref[0] == 1
    count = off_ref.shape[0]

    def extended(i, own):
        a, b = got0_ref[4 * i : 4 * i + 4, :], got1_ref[4 * i : 4 * i + 4, :]
        left, right = jnp.where(odd, a, b), jnp.where(odd, b, a)
        return jnp.concatenate([left, own, right], axis=0)

    eta = extended(0, ssh_ref[...])
    fresh = (fresh_gain / SUB) * extended(1, forcing_ref[(FIELDS - 1) * 8 :, :])
    lane = lax.broadcasted_iota(jnp.int32, (16, LANES), 1)
    places, crossing = [], []
    for j in range(count):
        target = lane + extended(2 + j, off_ref[j].astype(jnp.float32)).astype(jnp.int32)
        places.append(target & (LANES - 1))
        crossing.append((target < 0) | (target >= LANES))
    upper = lane >= LANES // 2
    for _ in range(SUB):
        beside = jnp.where(upper, pltpu.roll(eta, 1, 0), pltpu.roll(eta, 15, 0))
        halves = []
        for h in (0, 8):
            here, other = eta[h : h + 8], beside[h : h + 8]
            near = None
            for j in range(count):
                idx = places[j][h : h + 8]
                value = jnp.where(crossing[j][h : h + 8], pick(other, idx), pick(here, idx))
                near = value if near is None else near + value
            halves.append(near)
        average = jnp.concatenate(halves, axis=0) / 6.0
        eta = eta + relax_rate * (average - eta) + fresh
    height = eta[4:12]
    ssh_out[...] = height
    perm = perm_ref[...]
    out = permuted(height, perm >> 7, perm & (LANES - 1))
    for f, x in enumerate((top_ref[0], top_ref[1], out)):
        for d in range(8):
            state_out[d, f : f + 1, :] = x[d : d + 1]


def heights_and_state(odd, got0, got1, ssh, forcing, offs, top, perm):
    return pl.pallas_call(
        height_kernel,
        in_specs=[SMEM] + [VMEM] * 7,
        out_specs=[VMEM] * 2,
        out_shape=[shape_of((8, LANES)), shape_of((8, 3, LANES))],
        compiler_params=limit(4),
    )(odd, got0, got1, ssh, forcing, offs, top, perm)


def per_device(
    atm_flux,
    intersection_weight,
    src_block,
    dst_block,
    intersection_count,
    temp,
    kappa,
    ssh,
    nbr_offset,
    coupler_perm,
):
    tiles = lax.axis_size("tile")
    odd = (lax.axis_index("tile") % 2).astype(jnp.int32).reshape(1)
    height = ssh.reshape(8, LANES)
    perm = coupler_perm.reshape(8, LANES)
    temp, conduct = temp[0, 0], kappa.reshape(kappa.shape[2], 8, LANES)
    offsets = nbr_offset.reshape(nbr_offset.shape[2], 8, LANES)
    terms = remap_terms(src_block, intersection_count, atm_flux[0, 0], intersection_weight[0, 0])
    arrived = lax.all_to_all(terms, "comp", split_axis=0, concat_axis=0, tiled=True)
    onehot = one_hot_targets(terms, dst_block[0, 0])
    forcing, pay0, pay1 = forcing_and_halo(odd, arrived, onehot, height, offsets)
    inner = [(i, i ^ 1) for i in range(tiles)]
    outer = [(i, (i - 1 if i % 2 == 0 else i + 1) % tiles) for i in range(tiles)]
    got0 = lax.ppermute(pay0, "tile", inner)
    got1 = lax.ppermute(pay1, "tile", outer)
    top = surface_rows(temp, conduct, forcing, perm)
    height, state = heights_and_state(odd, got0, got1, height, forcing, offsets, top, perm)
    mixed = column_update(state, temp, conduct, forcing)
    relaid = lax.all_to_all(state, "comp", split_axis=0, concat_axis=0, tiled=True)
    coupler_state = relaid.transpose(1, 0, 2).reshape(1, 1, 3, -1)
    return (mixed[None, None], height.reshape(ssh.shape), coupler_state)


def solution(mesh):
    return jax.shard_map(
        per_device,
        mesh=mesh,
        in_specs=(
            P("comp", "tile", None, None),
            P("comp", "tile", None, None, None, None),
            P("comp", "tile", None, None),
            P("comp", "tile", None, None),
            P("comp", "tile", None, None),
            P("comp", "tile", None, None),
            P("comp", "tile", None, None),
            P("comp", "tile", None),
            P("comp", "tile", None, None),
            P("comp", "tile", None),
        ),
        out_specs=(
            P("comp", "tile", None, None),
            P("comp", "tile", None),
            P("comp", "tile", None, None),
        ),
        check_vma=False,
    )
```

```python
import functools
import math

import jax
import jax.numpy as jnp
from jax import lax
from jax.experimental import pallas as pl
from jax.experimental.pallas import tpu as pltpu
from jax.sharding import PartitionSpec as P

SUB = 8
MIX = 4
LANES = 128
FIELDS = 5

heat_gain = 0.5
shortwave_gain = 0.5
wind_mixing = 0.15
relax_rate = 0.5
fresh_gain = 0.5


def shape_of(dims, dtype=jnp.float32):
    return jax.ShapeDtypeStruct(dims, dtype)


def limit(mib):
    return pltpu.CompilerParams(vmem_limit_bytes=mib << 20)


def cost(flops, moved):
    return pl.CostEstimate(flops=flops, bytes_accessed=moved, transcendentals=0)


VMEM = pl.BlockSpec(memory_space=pltpu.VMEM)
SMEM = pl.BlockSpec(memory_space=pltpu.SMEM)
ANY = pl.BlockSpec(memory_space=pl.ANY)


def terms_kernel(
    src_hbm, cnt_hbm, flux_hbm, weight_hbm, out_hbm,
    src_ref, cnt_ref, flux_ref, blocks_ref, term_ref, held_ref, out_ref, sems, out_sems,
):
    groups, slots = weight_hbm.shape[:2]
    first = [
        pltpu.make_async_copy(src_hbm, src_ref, sems.at[groups]),
        pltpu.make_async_copy(cnt_hbm, cnt_ref, sems.at[groups + 1]),
        pltpu.make_async_copy(flux_hbm, flux_ref, sems.at[groups + 2]),
    ]
    copies = [
        pltpu.make_async_copy(weight_hbm.at[d], held_ref.at[d], sems.at[d]) for d in range(groups)
    ]
    results = [
        pltpu.make_async_copy(out_ref.at[d], out_hbm.at[d], out_sems.at[d]) for d in range(groups)
    ]
    for copy in first + copies:
        copy.start()
    for copy in first:
        copy.wait()
    for b in range(blocks_ref.shape[0]):
        blocks_ref[b] = flux_ref[:, b * LANES : (b + 1) * LANES].astype(jnp.float32)
    lane = lax.broadcasted_iota(jnp.int32, (8, LANES), 1)
    zero = jnp.zeros((8, LANES), jnp.float32)
    rest = out_ref.shape[1] - FIELDS * slots
    for d in range(groups):
        copies[d].wait()
        for k in range(0, slots, 2):
            parts = []
            for i in (0, 1):
                block = blocks_ref[src_ref[0, 0, d, k + i]]
                parts.append(jnp.where(lane < cnt_ref[0, 0, d, k + i], block, zero))
            top = jnp.concatenate([parts[0], zero], axis=1)
            low = jnp.concatenate([zero, parts[1]], axis=1)
            lhs = jnp.concatenate([top, low], axis=0).astype(jnp.bfloat16)
            rhs = held_ref[d, k : k + 2].reshape(2 * LANES, LANES)
            term_ref[d, k * 8 : k * 8 + 16, :] = jnp.dot(
                lhs, rhs, preferred_element_type=jnp.float32
            )
        f = [term_ref[d, pl.ds(i, slots, stride=8), :] for i in range(8)]
        for i, x in enumerate((f[1], f[0] + f[7], f[2], f[3], f[5] - f[4] + f[6])):
            out_ref[d, i * slots : (i + 1) * slots] = x
        if rest:
            out_ref[d, FIELDS * slots :] = jnp.zeros((rest, LANES), jnp.float32)
        results[d].start()
    for result in results:
        result.wait()


def remap_terms(src, cnt, flux, weights):
    groups, slots = weights.shape[:2]
    rows = -(-FIELDS * slots // 8) * 8
    return pl.pallas_call(
        terms_kernel,
        in_specs=[ANY] * 4,
        out_specs=ANY,
        out_shape=shape_of((groups, rows, LANES)),
        scratch_shapes=[
            pltpu.SMEM(src.shape, jnp.int32),
            pltpu.SMEM(cnt.shape, jnp.int32),
            pltpu.VMEM(flux.shape, flux.dtype),
            pltpu.VMEM((flux.shape[1] // LANES, 8, LANES), jnp.float32),
            pltpu.VMEM((groups, slots * 8, LANES), jnp.float32),
            pltpu.VMEM(weights.shape, weights.dtype),
            pltpu.VMEM((groups, rows, LANES), jnp.float32),
            pltpu.SemaphoreType.DMA((groups + 3,)),
            pltpu.SemaphoreType.DMA((groups,)),
        ],
    )(src, cnt, flux, weights)


def target_kernel(after_ref, dst_ref, out_ref, *, rows):
    groups, slots = dst_ref.shape
    dst = dst_ref[...]
    parts = [dst + 8 * f for f in range(FIELDS)]
    rest = rows - FIELDS * slots
    if rest:
        parts.append(jnp.full((groups, rest), -1, jnp.int32))
    ids = jnp.concatenate(parts, axis=1)
    line = jnp.concatenate([ids[c : c + 1, :] for c in range(groups)], axis=1)
    targets = lax.broadcasted_iota(jnp.int32, out_ref.shape, 0)
    hit = jnp.broadcast_to(line, out_ref.shape) == targets
    out_ref[...] = hit.astype(jnp.float32).astype(jnp.bfloat16)


def one_hot_targets(after, dst):
    groups, rows, _ = after.shape
    return pl.pallas_call(
        functools.partial(target_kernel, rows=rows),
        in_specs=[ANY, VMEM],
        out_specs=VMEM,
        out_shape=shape_of((48, groups * rows), jnp.bfloat16),
        cost_estimate=cost(1 << 20, 1 << 20),
        compiler_params=limit(4),
    )(after, dst)


def forcing_kernel(place_ref, arrived_ref, onehot_ref, ssh_ref, off_ref, forcing_ref, pay0_ref, pay1_ref, pay2_ref):
    onehot = onehot_ref[...]
    rest = arrived_ref[...].reshape(-1, LANES)
    total = None
    for _ in range(3):
        piece = rest.astype(jnp.bfloat16)
        part = jnp.dot(onehot, piece, preferred_element_type=jnp.float32)
        total = part if total is None else total + part
        rest = rest - piece.astype(jnp.float32)
    forcing_ref[...] = total[: FIELDS * 8]
    odd = place_ref[0] % 2 == 1
    pieces = [ssh_ref[...], total[(FIELDS - 1) * 8 : FIELDS * 8]]
    pieces += [off_ref[j].astype(jnp.float32) for j in range(off_ref.shape[0])]
    for i, x in enumerate(pieces):
        pay0_ref[4 * i : 4 * i + 4, :] = jnp.where(odd, x[0:4], x[4:8])
        pay1_ref[4 * i : 4 * i + 4, :] = jnp.where(odd, x[4:8], x[0:4])
        pay2_ref[4 * i : 4 * i + 4, :] = jnp.where(odd, x[0:4], x[4:8])


def forcing_and_halo(place, arrived, onehot, ssh, offsets):
    pay = shape_of((4 * (2 + offsets.shape[0]), LANES))
    return pl.pallas_call(
        forcing_kernel,
        in_specs=[SMEM] + [VMEM] * 4,
        out_specs=[VMEM] * 4,
        out_shape=[shape_of((FIELDS * 8, LANES)), pay, pay, pay],
        compiler_params=limit(4),
    )(place, arrived, onehot, ssh, offsets)


def column_parts(forcing_ref):
    east, north = forcing_ref[16:24, :], forcing_ref[24:32, :]
    mixing = wind_mixing * jnp.tanh(jnp.sqrt(east * east + north * north))
    return shortwave_gain * forcing_ref[0:8, :], heat_gain * forcing_ref[8:16, :], mixing


def mix_levels(kappa_ref, forcing_ref, tile_ref, levels):
    short, top, mixing = column_parts(forcing_ref)
    heated, keff = [], []
    for level in range(levels):
        shallow = math.exp(-level / 4.0) - math.exp(-(level + 1.0) / 4.0)
        value = tile_ref[level * 8 : level * 8 + 8, :] + short * shallow
        heated.append(value + top if level == 0 else value)
        if level < levels - 1:
            keff.append(kappa_ref[level] + mixing * math.exp(-level / 4.0))
    for _ in range(MIX):
        above = None
        for level in range(levels):
            here = heated[level]
            if level < levels - 1:
                below = keff[level] * (heated[level + 1] - here)
                new = here + below
            else:
                new = here
            heated[level] = new if above is None else new - above
            above = below
    return heated


def permuted(x, row, col):
    out = jnp.zeros((8, LANES), jnp.float32)
    for s in range(8):
        out = jnp.where(row == s, pick(jnp.broadcast_to(x[s : s + 1, :], (8, LANES)), col), out)
    return out


def pick(x, idx):
    return jnp.take_along_axis(x, idx, axis=1, mode="promise_in_bounds")


def surface_kernel(temp_ref, kappa_ref, forcing_ref, perm_ref, out_ref, tile_ref):
    for b in range(8):
        tile_ref[pl.ds(b, 8, stride=8), :] = temp_ref[:, b * LANES : (b + 1) * LANES]
    heated = mix_levels(kappa_ref, forcing_ref, tile_ref, MIX + 3)
    perm = perm_ref[...]
    row, col = perm >> 7, perm & (LANES - 1)
    for f in (0, 1):
        out_ref[f] = permuted(heated[f], row, col)


def surface_rows(temp, kappa, forcing, perm):
    return pl.pallas_call(
        surface_kernel,
        grid=(1,),
        in_specs=[
            pl.BlockSpec((8, temp.shape[1]), lambda i: (0, 0)),
            pl.BlockSpec((8, 8, LANES), lambda i: (0, 0, 0)),
            pl.BlockSpec(forcing.shape, lambda i: (0, 0)),
            pl.BlockSpec(perm.shape, lambda i: (0, 0)),
        ],
        out_specs=pl.BlockSpec((2, 8, LANES), lambda i: (0, 0, 0)),
        out_shape=shape_of((2, 8, LANES)),
        scratch_shapes=[pltpu.VMEM((64, LANES), jnp.float32)],
        cost_estimate=cost(1 << 20, 1 << 20),
        compiler_params=limit(4),
    )(temp, kappa, forcing, perm)


def column_kernel(height_ref, temp_ref, kappa_ref, forcing_ref, mixed_ref, ssh_out, tile_ref):
    ssh_out[...] = height_ref[...]
    levels = temp_ref.shape[0]
    for b in range(8):
        tile_ref[pl.ds(b, levels, stride=8), :] = temp_ref[:, b * LANES : (b + 1) * LANES]
    heated = mix_levels(kappa_ref, forcing_ref, tile_ref, levels)
    for level in range(levels):
        tile_ref[level * 8 : level * 8 + 8, :] = heated[level]
    for b in range(8):
        mixed_ref[:, b * LANES : (b + 1) * LANES] = tile_ref[pl.ds(b, levels, stride=8), :]


def column_update(height, temp, kappa, forcing):
    return pl.pallas_call(
        column_kernel,
        in_specs=[VMEM] * 4,
        out_specs=[VMEM] * 2,
        out_shape=[shape_of(temp.shape), shape_of(height.shape)],
        scratch_shapes=[pltpu.VMEM((temp.shape[0] * 8, LANES), jnp.float32)],
        cost_estimate=cost(1 << 22, 1 << 22),
        compiler_params=limit(4),
    )(height, temp, kappa, forcing)


def height_kernel(place_ref, got0_ref, got1_ref, got2_ref, ssh_ref, forcing_ref, off_ref, top_ref, perm_ref, ssh_out, state_out):
    odd, late = place_ref[0] % 2 == 1, place_ref[0] >= 2
    count = off_ref.shape[0]

    def extended(i, own):
        rows = slice(4 * i, 4 * i + 4)
        a, b = jnp.where(late, got2_ref[rows, :], got0_ref[rows, :]), got1_ref[rows, :]
        left, right = jnp.where(odd, a, b), jnp.where(odd, b, a)
        return jnp.concatenate([left, own, right], axis=0)

    eta = extended(0, ssh_ref[...])
    fresh = (fresh_gain / SUB) * extended(1, forcing_ref[(FIELDS - 1) * 8 :, :])
    lane = lax.broadcasted_iota(jnp.int32, (16, LANES), 1)
    places, crossing = [], []
    for j in range(count):
        target = lane + extended(2 + j, off_ref[j].astype(jnp.float32)).astype(jnp.int32)
        places.append(target & (LANES - 1))
        crossing.append((target < 0) | (target >= LANES))
    upper = lane >= LANES // 2
    for _ in range(SUB):
        kept = (1.0 - relax_rate) * eta + fresh
        beside = jnp.where(upper, pltpu.roll(eta, 1, 0), pltpu.roll(eta, 15, 0))
        halves = []
        for h in (0, 8):
            here, other = eta[h : h + 8], beside[h : h + 8]
            near = []
            for j in range(count):
                idx = places[j][h : h + 8]
                near.append(jnp.where(crossing[j][h : h + 8], pick(other, idx), pick(here, idx)))
            while len(near) > 1:
                near = [sum(near[i : i + 2]) for i in range(0, len(near), 2)]
            halves.append(near[0])
        eta = kept + (relax_rate / count) * jnp.concatenate(halves, axis=0)
    height = eta[4:12]
    ssh_out[...] = height
    perm = perm_ref[...]
    out = permuted(height, perm >> 7, perm & (LANES - 1))
    for f, x in enumerate((top_ref[0], top_ref[1], out)):
        for d in range(8):
            state_out[d, f : f + 1, :] = x[d : d + 1]


def heights_and_state(place, got0, got1, got2, ssh, forcing, offs, top, perm):
    return pl.pallas_call(
        height_kernel,
        in_specs=[SMEM] + [VMEM] * 8,
        out_specs=[VMEM] * 2,
        out_shape=[pltpu.VMEM((8, LANES), jnp.float32), pltpu.VMEM((8, 3, LANES), jnp.float32)],
        compiler_params=limit(4),
    )(place, got0, got1, got2, ssh, forcing, offs, top, perm)


def per_device(
    atm_flux,
    intersection_weight,
    src_block,
    dst_block,
    intersection_count,
    temp,
    kappa,
    ssh,
    nbr_offset,
    coupler_perm,
):
    tiles = lax.axis_size("tile")
    tile = lax.axis_index("tile")
    place = (tile % 2 + 2 * (tile % 24 >= 22)).astype(jnp.int32).reshape(1)
    height = ssh.reshape(8, LANES)
    perm = coupler_perm.reshape(8, LANES)
    temp, conduct = temp[0, 0], kappa.reshape(kappa.shape[2], 8, LANES)
    offsets = nbr_offset.reshape(nbr_offset.shape[2], 8, LANES)
    terms = remap_terms(src_block, intersection_count, atm_flux[0, 0], intersection_weight[0, 0])
    arrived = lax.all_to_all(terms, "comp", split_axis=0, concat_axis=0, tiled=True)
    onehot = one_hot_targets(terms, dst_block[0, 0])
    forcing, pay0, pay1, pay2 = forcing_and_halo(place, arrived, onehot, height, offsets)
    late = [i for i in range(tiles) if i % 24 >= 22]
    inner = [(i, i ^ 1) for i in range(tiles) if i not in late]
    inner_late = [(i, i ^ 1) for i in late]
    outer = [(i, (i - 1 if i % 2 == 0 else i + 1) % tiles) for i in range(tiles)]
    got0 = lax.ppermute(pay0, "tile", inner)
    got1 = lax.ppermute(pay1, "tile", outer)
    got2 = lax.ppermute(pay2, "tile", inner_late)
    top = surface_rows(temp, conduct, forcing, perm)
    height, state = heights_and_state(place, got0, got1, got2, height, forcing, offsets, top, perm)
    mixed, height = column_update(height, temp, conduct, forcing)
    relaid = lax.all_to_all(state, "comp", split_axis=0, concat_axis=0, tiled=True)
    coupler_state = relaid.transpose(1, 0, 2).reshape(1, 1, 3, -1)
    return (mixed[None, None], height.reshape(ssh.shape), coupler_state)


def solution(mesh):
    return jax.shard_map(
        per_device,
        mesh=mesh,
        in_specs=(
            P("comp", "tile", None, None),
            P("comp", "tile", None, None, None, None),
            P("comp", "tile", None, None),
            P("comp", "tile", None, None),
            P("comp", "tile", None, None),
            P("comp", "tile", None, None),
            P("comp", "tile", None, None),
            P("comp", "tile", None),
            P("comp", "tile", None, None),
            P("comp", "tile", None),
        ),
        out_specs=(
            P("comp", "tile", None, None),
            P("comp", "tile", None),
            P("comp", "tile", None, None),
        ),
        check_vma=False,
    )
```

```python
import functools
import math

import jax
import jax.numpy as jnp
from jax import lax
from jax.experimental import pallas as pl
from jax.experimental.pallas import tpu as pltpu
from jax.sharding import PartitionSpec as P

SUB = 8
MIX = 4
LANES = 128
FIELDS = 5
TERMS_FIRST = 6
STATE_FIRST = 4

heat_gain = 0.5
shortwave_gain = 0.5
wind_mixing = 0.15
relax_rate = 0.5
fresh_gain = 0.5


def shape_of(dims, dtype=jnp.float32):
    return jax.ShapeDtypeStruct(dims, dtype)


def over_groups(x, groups, first):
    order = [[(i + first) % groups for i in range(groups)]]
    return lax.all_to_all(
        x, "comp", split_axis=0, concat_axis=0, axis_index_groups=order, tiled=True
    )


def limit(mib):
    return pltpu.CompilerParams(vmem_limit_bytes=mib << 20)


def cost(flops, moved):
    return pl.CostEstimate(flops=flops, bytes_accessed=moved, transcendentals=0)


VMEM = pl.BlockSpec(memory_space=pltpu.VMEM)
SMEM = pl.BlockSpec(memory_space=pltpu.SMEM)
ANY = pl.BlockSpec(memory_space=pl.ANY)


def terms_kernel(
    src_hbm, cnt_hbm, flux_hbm, weight_hbm, out_hbm,
    src_ref, cnt_ref, flux_ref, blocks_ref, term_ref, held_ref, out_ref, sems, out_sems,
):
    groups, slots = weight_hbm.shape[:2]
    first = [
        pltpu.make_async_copy(src_hbm, src_ref, sems.at[groups]),
        pltpu.make_async_copy(cnt_hbm, cnt_ref, sems.at[groups + 1]),
        pltpu.make_async_copy(flux_hbm, flux_ref, sems.at[groups + 2]),
    ]
    copies = [
        pltpu.make_async_copy(weight_hbm.at[d], held_ref.at[d], sems.at[d]) for d in range(groups)
    ]
    results = [
        pltpu.make_async_copy(out_ref.at[d], out_hbm.at[(d - TERMS_FIRST) % groups], out_sems.at[d])
        for d in range(groups)
    ]
    for copy in first + copies:
        copy.start()
    for copy in first:
        copy.wait()
    for b in range(blocks_ref.shape[0]):
        blocks_ref[b] = flux_ref[:, b * LANES : (b + 1) * LANES].astype(jnp.float32)
    lane = lax.broadcasted_iota(jnp.int32, (8, LANES), 1)
    zero = jnp.zeros((8, LANES), jnp.float32)
    rest = out_ref.shape[1] - FIELDS * slots
    for d in range(groups):
        copies[d].wait()
        for k in range(0, slots, 2):
            parts = []
            for i in (0, 1):
                block = blocks_ref[src_ref[0, 0, d, k + i]]
                parts.append(jnp.where(lane < cnt_ref[0, 0, d, k + i], block, zero))
            top = jnp.concatenate([parts[0], zero], axis=1)
            low = jnp.concatenate([zero, parts[1]], axis=1)
            lhs = jnp.concatenate([top, low], axis=0).astype(jnp.bfloat16)
            rhs = held_ref[d, k : k + 2].reshape(2 * LANES, LANES)
            term_ref[d, k * 8 : k * 8 + 16, :] = jnp.dot(
                lhs, rhs, preferred_element_type=jnp.float32
            )
        f = [term_ref[d, pl.ds(i, slots, stride=8), :] for i in range(8)]
        for i, x in enumerate((f[1], f[0] + f[7], f[2], f[3], f[5] - f[4] + f[6])):
            out_ref[d, i * slots : (i + 1) * slots] = x
        if rest:
            out_ref[d, FIELDS * slots :] = jnp.zeros((rest, LANES), jnp.float32)
        results[d].start()
    for result in results:
        result.wait()


def remap_terms(src, cnt, flux, weights):
    groups, slots = weights.shape[:2]
    rows = -(-FIELDS * slots // 8) * 8
    return pl.pallas_call(
        terms_kernel,
        in_specs=[ANY] * 4,
        out_specs=ANY,
        out_shape=shape_of((groups, rows, LANES)),
        scratch_shapes=[
            pltpu.SMEM(src.shape, jnp.int32),
            pltpu.SMEM(cnt.shape, jnp.int32),
            pltpu.VMEM(flux.shape, flux.dtype),
            pltpu.VMEM((flux.shape[1] // LANES, 8, LANES), jnp.float32),
            pltpu.VMEM((groups, slots * 8, LANES), jnp.float32),
            pltpu.VMEM(weights.shape, weights.dtype),
            pltpu.VMEM((groups, rows, LANES), jnp.float32),
            pltpu.SemaphoreType.DMA((groups + 3,)),
            pltpu.SemaphoreType.DMA((groups,)),
        ],
    )(src, cnt, flux, weights)


def target_kernel(after_ref, dst_ref, out_ref, *, rows):
    groups, slots = dst_ref.shape
    dst = dst_ref[...]
    parts = [dst + 8 * f for f in range(FIELDS)]
    rest = rows - FIELDS * slots
    if rest:
        parts.append(jnp.full((groups, rest), -1, jnp.int32))
    ids = jnp.concatenate(parts, axis=1)
    in_order = [(i + TERMS_FIRST) % groups for i in range(groups)]
    line = jnp.concatenate([ids[c : c + 1, :] for c in in_order], axis=1)
    targets = lax.broadcasted_iota(jnp.int32, out_ref.shape, 0)
    hit = jnp.broadcast_to(line, out_ref.shape) == targets
    out_ref[...] = hit.astype(jnp.float32).astype(jnp.bfloat16)


def one_hot_targets(after, dst):
    groups, rows, _ = after.shape
    return pl.pallas_call(
        functools.partial(target_kernel, rows=rows),
        in_specs=[ANY, VMEM],
        out_specs=VMEM,
        out_shape=shape_of((48, groups * rows), jnp.bfloat16),
        cost_estimate=cost(1 << 20, 1 << 20),
        compiler_params=limit(4),
    )(after, dst)


def forcing_kernel(place_ref, arrived_ref, onehot_ref, ssh_ref, off_ref, forcing_ref, pay0_ref, pay1_ref, pay2_ref):
    onehot = onehot_ref[...]
    rest = arrived_ref[...].reshape(-1, LANES)
    total = None
    for _ in range(3):
        piece = rest.astype(jnp.bfloat16)
        part = jnp.dot(onehot, piece, preferred_element_type=jnp.float32)
        total = part if total is None else total + part
        rest = rest - piece.astype(jnp.float32)
    forcing_ref[...] = total[: FIELDS * 8]
    odd = place_ref[0] % 2 == 1
    pieces = [ssh_ref[...], total[(FIELDS - 1) * 8 : FIELDS * 8]]
    pieces += [off_ref[j].astype(jnp.float32) for j in range(off_ref.shape[0])]
    for i, x in enumerate(pieces):
        pay0_ref[4 * i : 4 * i + 4, :] = jnp.where(odd, x[0:4], x[4:8])
        pay1_ref[4 * i : 4 * i + 4, :] = jnp.where(odd, x[4:8], x[0:4])
        pay2_ref[4 * i : 4 * i + 4, :] = jnp.where(odd, x[0:4], x[4:8])


def forcing_and_halo(place, arrived, onehot, ssh, offsets):
    pay = shape_of((4 * (2 + offsets.shape[0]), LANES))
    return pl.pallas_call(
        forcing_kernel,
        in_specs=[SMEM] + [VMEM] * 4,
        out_specs=[VMEM] * 4,
        out_shape=[shape_of((FIELDS * 8, LANES)), pay, pay, pay],
        compiler_params=limit(4),
    )(place, arrived, onehot, ssh, offsets)


def column_parts(forcing_ref):
    east, north = forcing_ref[16:24, :], forcing_ref[24:32, :]
    mixing = wind_mixing * jnp.tanh(jnp.sqrt(east * east + north * north))
    return shortwave_gain * forcing_ref[0:8, :], heat_gain * forcing_ref[8:16, :], mixing


def mix_levels(kappa_ref, forcing_ref, tile_ref, levels):
    short, top, mixing = column_parts(forcing_ref)
    heated, keff = [], []
    for level in range(levels):
        shallow = math.exp(-level / 4.0) - math.exp(-(level + 1.0) / 4.0)
        value = tile_ref[level * 8 : level * 8 + 8, :] + short * shallow
        heated.append(value + top if level == 0 else value)
        if level < levels - 1:
            keff.append(kappa_ref[level] + mixing * math.exp(-level / 4.0))
    for _ in range(MIX):
        above = None
        for level in range(levels):
            here = heated[level]
            if level < levels - 1:
                below = keff[level] * (heated[level + 1] - here)
                new = here + below
            else:
                new = here
            heated[level] = new if above is None else new - above
            above = below
    return heated


def permuted(x, row, col):
    out = jnp.zeros((8, LANES), jnp.float32)
    for s in range(8):
        out = jnp.where(row == s, pick(jnp.broadcast_to(x[s : s + 1, :], (8, LANES)), col), out)
    return out


def pick(x, idx):
    return jnp.take_along_axis(x, idx, axis=1, mode="promise_in_bounds")


def surface_kernel(temp_ref, kappa_ref, forcing_ref, perm_ref, out_ref, tile_ref):
    for b in range(8):
        tile_ref[pl.ds(b, 8, stride=8), :] = temp_ref[:, b * LANES : (b + 1) * LANES]
    heated = mix_levels(kappa_ref, forcing_ref, tile_ref, MIX + 3)
    perm = perm_ref[...]
    row, col = perm >> 7, perm & (LANES - 1)
    for f in (0, 1):
        out_ref[f] = permuted(heated[f], row, col)


def surface_rows(temp, kappa, forcing, perm):
    return pl.pallas_call(
        surface_kernel,
        grid=(1,),
        in_specs=[
            pl.BlockSpec((8, temp.shape[1]), lambda i: (0, 0)),
            pl.BlockSpec((8, 8, LANES), lambda i: (0, 0, 0)),
            pl.BlockSpec(forcing.shape, lambda i: (0, 0)),
            pl.BlockSpec(perm.shape, lambda i: (0, 0)),
        ],
        out_specs=pl.BlockSpec((2, 8, LANES), lambda i: (0, 0, 0)),
        out_shape=shape_of((2, 8, LANES)),
        scratch_shapes=[pltpu.VMEM((64, LANES), jnp.float32)],
        cost_estimate=cost(1 << 20, 1 << 20),
        compiler_params=limit(4),
    )(temp, kappa, forcing, perm)


def column_kernel(height_ref, temp_ref, kappa_ref, forcing_ref, mixed_ref, ssh_out, tile_ref):
    ssh_out[...] = height_ref[...]
    levels = temp_ref.shape[0]
    for b in range(8):
        tile_ref[pl.ds(b, levels, stride=8), :] = temp_ref[:, b * LANES : (b + 1) * LANES]
    heated = mix_levels(kappa_ref, forcing_ref, tile_ref, levels)
    for level in range(levels):
        tile_ref[level * 8 : level * 8 + 8, :] = heated[level]
    for b in range(8):
        mixed_ref[:, b * LANES : (b + 1) * LANES] = tile_ref[pl.ds(b, levels, stride=8), :]


def column_update(height, temp, kappa, forcing):
    return pl.pallas_call(
        column_kernel,
        in_specs=[VMEM] * 4,
        out_specs=[VMEM] * 2,
        out_shape=[shape_of(temp.shape), shape_of(height.shape)],
        scratch_shapes=[pltpu.VMEM((temp.shape[0] * 8, LANES), jnp.float32)],
        cost_estimate=cost(1 << 22, 1 << 22),
        compiler_params=limit(4),
    )(height, temp, kappa, forcing)


def height_kernel(place_ref, got0_ref, got1_ref, got2_ref, ssh_ref, forcing_ref, off_ref, top_ref, perm_ref, ssh_out, state_out):
    odd, late = place_ref[0] % 2 == 1, place_ref[0] >= 2
    count = off_ref.shape[0]

    def extended(i, own):
        rows = slice(4 * i, 4 * i + 4)
        a, b = jnp.where(late, got2_ref[rows, :], got0_ref[rows, :]), got1_ref[rows, :]
        left, right = jnp.where(odd, a, b), jnp.where(odd, b, a)
        return jnp.concatenate([left, own, right], axis=0)

    eta = extended(0, ssh_ref[...])
    fresh = (fresh_gain / SUB) * extended(1, forcing_ref[(FIELDS - 1) * 8 :, :])
    lane = lax.broadcasted_iota(jnp.int32, (16, LANES), 1)
    places, crossing = [], []
    for j in range(count):
        target = lane + extended(2 + j, off_ref[j].astype(jnp.float32)).astype(jnp.int32)
        places.append(target & (LANES - 1))
        crossing.append((target < 0) | (target >= LANES))
    upper = lane >= LANES // 2
    for _ in range(SUB):
        kept = (1.0 - relax_rate) * eta + fresh
        beside = jnp.where(upper, pltpu.roll(eta, 1, 0), pltpu.roll(eta, 15, 0))
        halves = []
        for h in (0, 8):
            here, other = eta[h : h + 8], beside[h : h + 8]
            near = []
            for j in range(count):
                idx = places[j][h : h + 8]
                near.append(jnp.where(crossing[j][h : h + 8], pick(other, idx), pick(here, idx)))
            while len(near) > 1:
                near = [sum(near[i : i + 2]) for i in range(0, len(near), 2)]
            halves.append(near[0])
        eta = kept + (relax_rate / count) * jnp.concatenate(halves, axis=0)
    height = eta[4:12]
    ssh_out[...] = height
    perm = perm_ref[...]
    out = permuted(height, perm >> 7, perm & (LANES - 1))
    for f, x in enumerate((top_ref[0], top_ref[1], out)):
        for d in range(8):
            state_out[(d - STATE_FIRST) % 8, f : f + 1, :] = x[d : d + 1]


def heights_and_state(place, got0, got1, got2, ssh, forcing, offs, top, perm):
    return pl.pallas_call(
        height_kernel,
        in_specs=[SMEM] + [VMEM] * 8,
        out_specs=[VMEM] * 2,
        out_shape=[pltpu.VMEM((8, LANES), jnp.float32), pltpu.VMEM((8, 3, LANES), jnp.float32)],
        compiler_params=limit(4),
    )(place, got0, got1, got2, ssh, forcing, offs, top, perm)


def per_device(
    atm_flux,
    intersection_weight,
    src_block,
    dst_block,
    intersection_count,
    temp,
    kappa,
    ssh,
    nbr_offset,
    coupler_perm,
):
    tiles, groups = lax.axis_size("tile"), lax.axis_size("comp")
    tile = lax.axis_index("tile")
    place = (tile % 2 + 2 * (tile % 24 >= 22)).astype(jnp.int32).reshape(1)
    height = ssh.reshape(8, LANES)
    perm = coupler_perm.reshape(8, LANES)
    temp, conduct = temp[0, 0], kappa.reshape(kappa.shape[2], 8, LANES)
    offsets = nbr_offset.reshape(nbr_offset.shape[2], 8, LANES)
    terms = remap_terms(src_block, intersection_count, atm_flux[0, 0], intersection_weight[0, 0])
    arrived = over_groups(terms, groups, TERMS_FIRST)
    onehot = one_hot_targets(terms, dst_block[0, 0])
    forcing, pay0, pay1, pay2 = forcing_and_halo(place, arrived, onehot, height, offsets)
    late = [i for i in range(tiles) if i % 24 >= 22]
    inner = [(i, i ^ 1) for i in range(tiles) if i not in late]
    inner_late = [(i, i ^ 1) for i in late]
    outer = [(i, (i - 1 if i % 2 == 0 else i + 1) % tiles) for i in range(tiles)]
    got0 = lax.ppermute(pay0, "tile", inner)
    got1 = lax.ppermute(pay1, "tile", outer)
    got2 = lax.ppermute(pay2, "tile", inner_late)
    top = surface_rows(temp, conduct, forcing, perm)
    height, state = heights_and_state(place, got0, got1, got2, height, forcing, offsets, top, perm)
    mixed, height = column_update(height, temp, conduct, forcing)
    relaid = over_groups(state, groups, STATE_FIRST)
    relaid = jnp.roll(relaid, STATE_FIRST, axis=0)
    coupler_state = relaid.transpose(1, 0, 2).reshape(1, 1, 3, -1)
    return (mixed[None, None], height.reshape(ssh.shape), coupler_state)


def solution(mesh):
    return jax.shard_map(
        per_device,
        mesh=mesh,
        in_specs=(
            P("comp", "tile", None, None),
            P("comp", "tile", None, None, None, None),
            P("comp", "tile", None, None),
            P("comp", "tile", None, None),
            P("comp", "tile", None, None),
            P("comp", "tile", None, None),
            P("comp", "tile", None, None),
            P("comp", "tile", None),
            P("comp", "tile", None, None),
            P("comp", "tile", None),
        ),
        out_specs=(
            P("comp", "tile", None, None),
            P("comp", "tile", None),
            P("comp", "tile", None, None),
        ),
        check_vma=False,
    )
```

```python
import functools
import math

import jax
import jax.numpy as jnp
from jax import lax
from jax.experimental import pallas as pl
from jax.experimental.pallas import tpu as pltpu
from jax.sharding import PartitionSpec as P

SUB = 8
MIX = 4
LANES = 128
FIELDS = 5
TERMS_FIRST = 6
STATE_FIRST = 4

heat_gain = 0.5
shortwave_gain = 0.5
wind_mixing = 0.15
relax_rate = 0.5
fresh_gain = 0.5


def shape_of(dims, dtype=jnp.float32):
    return jax.ShapeDtypeStruct(dims, dtype)


def over_groups(x, groups, first):
    order = [[(i + first) % groups for i in range(groups)]]
    return lax.all_to_all(
        x, "comp", split_axis=0, concat_axis=0, axis_index_groups=order, tiled=True
    )


def limit(mib):
    return pltpu.CompilerParams(vmem_limit_bytes=mib << 20)


def cost(flops, moved):
    return pl.CostEstimate(flops=flops, bytes_accessed=moved, transcendentals=0)


VMEM = pl.BlockSpec(memory_space=pltpu.VMEM)
SMEM = pl.BlockSpec(memory_space=pltpu.SMEM)
ANY = pl.BlockSpec(memory_space=pl.ANY)


def terms_kernel(
    src_hbm, cnt_hbm, flux_hbm, weight_hbm, out_hbm,
    src_ref, cnt_ref, flux_ref, blocks_ref, term_ref, held_ref, out_ref, sems, out_sems,
):
    groups, slots = weight_hbm.shape[:2]
    first = [
        pltpu.make_async_copy(src_hbm, src_ref, sems.at[groups]),
        pltpu.make_async_copy(cnt_hbm, cnt_ref, sems.at[groups + 1]),
        pltpu.make_async_copy(flux_hbm, flux_ref, sems.at[groups + 2]),
    ]
    copies = [
        pltpu.make_async_copy(weight_hbm.at[d], held_ref.at[d], sems.at[d]) for d in range(groups)
    ]
    results = [
        pltpu.make_async_copy(out_ref.at[d], out_hbm.at[(d - TERMS_FIRST) % groups], out_sems.at[d])
        for d in range(groups)
    ]
    for copy in first + copies:
        copy.start()
    for copy in first:
        copy.wait()
    for b in range(blocks_ref.shape[0]):
        blocks_ref[b] = flux_ref[:, b * LANES : (b + 1) * LANES].astype(jnp.float32)
    lane = lax.broadcasted_iota(jnp.int32, (8, LANES), 1)
    zero = jnp.zeros((8, LANES), jnp.float32)
    rest = out_ref.shape[1] - FIELDS * slots
    for d in range(groups):
        copies[d].wait()
        for k in range(0, slots, 2):
            parts = []
            for i in (0, 1):
                block = blocks_ref[src_ref[0, 0, d, k + i]]
                parts.append(jnp.where(lane < cnt_ref[0, 0, d, k + i], block, zero))
            top = jnp.concatenate([parts[0], zero], axis=1)
            low = jnp.concatenate([zero, parts[1]], axis=1)
            lhs = jnp.concatenate([top, low], axis=0).astype(jnp.bfloat16)
            rhs = held_ref[d, k : k + 2].reshape(2 * LANES, LANES)
            term_ref[d, k * 8 : k * 8 + 16, :] = jnp.dot(
                lhs, rhs, preferred_element_type=jnp.float32
            )
        f = [term_ref[d, pl.ds(i, slots, stride=8), :] for i in range(8)]
        for i, x in enumerate((f[1], f[0] + f[7], f[2], f[3], f[5] - f[4] + f[6])):
            out_ref[d, i * slots : (i + 1) * slots] = x
        if rest:
            out_ref[d, FIELDS * slots :] = jnp.zeros((rest, LANES), jnp.float32)
        results[d].start()
    for result in results:
        result.wait()


def remap_terms(src, cnt, flux, weights):
    groups, slots = weights.shape[:2]
    rows = -(-FIELDS * slots // 8) * 8
    return pl.pallas_call(
        terms_kernel,
        in_specs=[ANY] * 4,
        out_specs=ANY,
        out_shape=shape_of((groups, rows, LANES)),
        scratch_shapes=[
            pltpu.SMEM(src.shape, jnp.int32),
            pltpu.SMEM(cnt.shape, jnp.int32),
            pltpu.VMEM(flux.shape, flux.dtype),
            pltpu.VMEM((flux.shape[1] // LANES, 8, LANES), jnp.float32),
            pltpu.VMEM((groups, slots * 8 + 8, LANES), jnp.float32),
            pltpu.VMEM(weights.shape, weights.dtype),
            pltpu.VMEM((groups, rows, LANES), jnp.float32),
            pltpu.SemaphoreType.DMA((groups + 3,)),
            pltpu.SemaphoreType.DMA((groups,)),
        ],
    )(src, cnt, flux, weights)


def target_kernel(after_ref, dst_ref, out_ref, *, rows):
    groups, slots = dst_ref.shape
    dst = dst_ref[...]
    parts = [dst + 8 * f for f in range(FIELDS)]
    rest = rows - FIELDS * slots
    if rest:
        parts.append(jnp.full((groups, rest), -1, jnp.int32))
    ids = jnp.concatenate(parts, axis=1)
    in_order = [(i + TERMS_FIRST) % groups for i in range(groups)]
    line = jnp.concatenate([ids[c : c + 1, :] for c in in_order], axis=1)
    targets = lax.broadcasted_iota(jnp.int32, out_ref.shape, 0)
    hit = jnp.broadcast_to(line, out_ref.shape) == targets
    out_ref[...] = hit.astype(jnp.float32).astype(jnp.bfloat16)


def one_hot_targets(after, dst):
    groups, rows, _ = after.shape
    return pl.pallas_call(
        functools.partial(target_kernel, rows=rows),
        in_specs=[ANY, VMEM],
        out_specs=VMEM,
        out_shape=shape_of((48, groups * rows), jnp.bfloat16),
        cost_estimate=cost(1 << 20, 1 << 20),
        compiler_params=limit(4),
    )(after, dst)


def forcing_kernel(place_ref, arrived_ref, onehot_ref, ssh_ref, off_ref, forcing_ref, pay0_ref, pay1_ref, pay2_ref):
    onehot = onehot_ref[...]
    rest = arrived_ref[...].reshape(-1, LANES)
    total = None
    for _ in range(3):
        piece = rest.astype(jnp.bfloat16)
        part = jnp.dot(onehot, piece, preferred_element_type=jnp.float32)
        total = part if total is None else total + part
        rest = rest - piece.astype(jnp.float32)
    forcing_ref[...] = total[: FIELDS * 8]
    odd = place_ref[0] % 2 == 1
    pieces = [ssh_ref[...], total[(FIELDS - 1) * 8 : FIELDS * 8]]
    pieces += [off_ref[j].astype(jnp.float32) for j in range(off_ref.shape[0])]
    for i, x in enumerate(pieces):
        pay0_ref[4 * i : 4 * i + 4, :] = jnp.where(odd, x[0:4], x[4:8])
        pay1_ref[4 * i : 4 * i + 4, :] = jnp.where(odd, x[4:8], x[0:4])
        pay2_ref[4 * i : 4 * i + 4, :] = jnp.where(odd, x[0:4], x[4:8])


def forcing_and_halo(place, arrived, onehot, ssh, offsets):
    pay = shape_of((4 * (2 + offsets.shape[0]), LANES))
    return pl.pallas_call(
        forcing_kernel,
        in_specs=[SMEM] + [VMEM] * 4,
        out_specs=[VMEM] * 4,
        out_shape=[shape_of((FIELDS * 8, LANES)), pay, pay, pay],
        compiler_params=limit(4),
    )(place, arrived, onehot, ssh, offsets)


def column_parts(forcing_ref):
    east, north = forcing_ref[16:24, :], forcing_ref[24:32, :]
    mixing = wind_mixing * jnp.tanh(jnp.sqrt(east * east + north * north))
    return shortwave_gain * forcing_ref[0:8, :], heat_gain * forcing_ref[8:16, :], mixing


def mix_levels(kappa_ref, forcing_ref, tile_ref, levels):
    short, top, mixing = column_parts(forcing_ref)
    heated, keff = [], []
    for level in range(levels):
        shallow = math.exp(-level / 4.0) - math.exp(-(level + 1.0) / 4.0)
        value = tile_ref[level * 8 : level * 8 + 8, :] + short * shallow
        heated.append(value + top if level == 0 else value)
        if level < levels - 1:
            keff.append(kappa_ref[level] + mixing * math.exp(-level / 4.0))
    for _ in range(MIX):
        above = None
        for level in range(levels):
            here = heated[level]
            if level < levels - 1:
                below = keff[level] * (heated[level + 1] - here)
                new = here + below
            else:
                new = here
            heated[level] = new if above is None else new - above
            above = below
    return heated


def permuted(x, row, col):
    out = jnp.zeros((8, LANES), jnp.float32)
    for s in range(8):
        out = jnp.where(row == s, pick(jnp.broadcast_to(x[s : s + 1, :], (8, LANES)), col), out)
    return out


def pick(x, idx):
    return jnp.take_along_axis(x, idx, axis=1, mode="promise_in_bounds")


def surface_kernel(temp_ref, kappa_ref, forcing_ref, perm_ref, out_ref, tile_ref):
    for b in range(8):
        tile_ref[pl.ds(b, 8, stride=8), :] = temp_ref[:, b * LANES : (b + 1) * LANES]
    heated = mix_levels(kappa_ref, forcing_ref, tile_ref, MIX + 3)
    perm = perm_ref[...]
    row, col = perm >> 7, perm & (LANES - 1)
    for f in (0, 1):
        out_ref[f] = permuted(heated[f], row, col)


def surface_rows(temp, kappa, forcing, perm):
    return pl.pallas_call(
        surface_kernel,
        grid=(1,),
        in_specs=[
            pl.BlockSpec((8, temp.shape[1]), lambda i: (0, 0)),
            pl.BlockSpec((8, 8, LANES), lambda i: (0, 0, 0)),
            pl.BlockSpec(forcing.shape, lambda i: (0, 0)),
            pl.BlockSpec(perm.shape, lambda i: (0, 0)),
        ],
        out_specs=pl.BlockSpec((2, 8, LANES), lambda i: (0, 0, 0)),
        out_shape=shape_of((2, 8, LANES)),
        scratch_shapes=[pltpu.VMEM((72, LANES), jnp.float32)],
        cost_estimate=cost(1 << 20, 1 << 20),
        compiler_params=limit(4),
    )(temp, kappa, forcing, perm)


def column_kernel(height_ref, temp_ref, kappa_ref, forcing_ref, mixed_ref, ssh_out, tile_ref):
    ssh_out[...] = height_ref[...]
    levels = temp_ref.shape[0]
    for b in range(8):
        tile_ref[pl.ds(b, levels, stride=8), :] = temp_ref[:, b * LANES : (b + 1) * LANES]
    heated = mix_levels(kappa_ref, forcing_ref, tile_ref, levels)
    for level in range(levels):
        tile_ref[level * 8 : level * 8 + 8, :] = heated[level]
    for b in range(8):
        mixed_ref[:, b * LANES : (b + 1) * LANES] = tile_ref[pl.ds(b, levels, stride=8), :]


def column_update(height, temp, kappa, forcing):
    return pl.pallas_call(
        column_kernel,
        in_specs=[VMEM] * 4,
        out_specs=[VMEM] * 2,
        out_shape=[shape_of(temp.shape), shape_of(height.shape)],
        scratch_shapes=[pltpu.VMEM((temp.shape[0] * 8 + 8, LANES), jnp.float32)],
        cost_estimate=cost(1 << 22, 1 << 22),
        compiler_params=limit(4),
    )(height, temp, kappa, forcing)


def height_kernel(place_ref, got0_ref, got1_ref, got2_ref, ssh_ref, forcing_ref, off_ref, top_ref, perm_ref, ssh_out, state_out):
    odd, late = place_ref[0] % 2 == 1, place_ref[0] >= 2
    count = off_ref.shape[0]

    def extended(i, own):
        rows = slice(4 * i, 4 * i + 4)
        a, b = jnp.where(late, got2_ref[rows, :], got0_ref[rows, :]), got1_ref[rows, :]
        left, right = jnp.where(odd, a, b), jnp.where(odd, b, a)
        return jnp.concatenate([left, own, right], axis=0)

    eta = extended(0, ssh_ref[...])
    fresh = (fresh_gain / SUB) * extended(1, forcing_ref[(FIELDS - 1) * 8 :, :])
    lane = lax.broadcasted_iota(jnp.int32, (16, LANES), 1)
    places, crossing = [], []
    for j in range(count):
        target = lane + extended(2 + j, off_ref[j].astype(jnp.float32)).astype(jnp.int32)
        places.append(target & (LANES - 1))
        crossing.append((target < 0) | (target >= LANES))
    upper = lane >= LANES // 2
    for _ in range(SUB):
        kept = (1.0 - relax_rate) * eta + fresh
        beside = jnp.where(upper, pltpu.roll(eta, 1, 0), pltpu.roll(eta, 15, 0))
        halves = []
        for h in (0, 8):
            here, other = eta[h : h + 8], beside[h : h + 8]
            near = []
            for j in range(count):
                idx = places[j][h : h + 8]
                near.append(jnp.where(crossing[j][h : h + 8], pick(other, idx), pick(here, idx)))
            while len(near) > 1:
                near = [sum(near[i : i + 2]) for i in range(0, len(near), 2)]
            halves.append(near[0])
        eta = kept + (relax_rate / count) * jnp.concatenate(halves, axis=0)
    height = eta[4:12]
    ssh_out[...] = height
    perm = perm_ref[...]
    out = permuted(height, perm >> 7, perm & (LANES - 1))
    for f, x in enumerate((top_ref[0], top_ref[1], out)):
        for d in range(8):
            state_out[(d - STATE_FIRST) % 8, f : f + 1, :] = x[d : d + 1]


def heights_and_state(place, got0, got1, got2, ssh, forcing, offs, top, perm):
    return pl.pallas_call(
        height_kernel,
        in_specs=[SMEM] + [VMEM] * 8,
        out_specs=[VMEM] * 2,
        out_shape=[pltpu.VMEM((8, LANES), jnp.float32), pltpu.VMEM((8, 3, LANES), jnp.float32)],
        compiler_params=limit(4),
    )(place, got0, got1, got2, ssh, forcing, offs, top, perm)


def per_device(
    atm_flux,
    intersection_weight,
    src_block,
    dst_block,
    intersection_count,
    temp,
    kappa,
    ssh,
    nbr_offset,
    coupler_perm,
):
    tiles, groups = lax.axis_size("tile"), lax.axis_size("comp")
    tile = lax.axis_index("tile")
    place = (tile % 2 + 2 * (tile % 24 >= 22)).astype(jnp.int32).reshape(1)
    height = ssh.reshape(8, LANES)
    perm = coupler_perm.reshape(8, LANES)
    temp, conduct = temp[0, 0], kappa.reshape(kappa.shape[2], 8, LANES)
    offsets = nbr_offset.reshape(nbr_offset.shape[2], 8, LANES)
    terms = remap_terms(src_block, intersection_count, atm_flux[0, 0], intersection_weight[0, 0])
    arrived = over_groups(terms, groups, TERMS_FIRST)
    onehot = one_hot_targets(terms, dst_block[0, 0])
    forcing, pay0, pay1, pay2 = forcing_and_halo(place, arrived, onehot, height, offsets)
    late = [i for i in range(tiles) if i % 24 >= 22]
    inner = [(i, i ^ 1) for i in range(tiles) if i not in late]
    inner_late = [(i, i ^ 1) for i in late]
    outer = [(i, (i - 1 if i % 2 == 0 else i + 1) % tiles) for i in range(tiles)]
    got0 = lax.ppermute(pay0, "tile", inner)
    got1 = lax.ppermute(pay1, "tile", outer)
    got2 = lax.ppermute(pay2, "tile", inner_late)
    top = surface_rows(temp, conduct, forcing, perm)
    height, state = heights_and_state(place, got0, got1, got2, height, forcing, offsets, top, perm)
    mixed, height = column_update(height, temp, conduct, forcing)
    relaid = over_groups(state, groups, STATE_FIRST)
    relaid = jnp.roll(relaid, STATE_FIRST, axis=0)
    coupler_state = relaid.transpose(1, 0, 2).reshape(1, 1, 3, -1)
    return (mixed[None, None], height.reshape(ssh.shape), coupler_state)


def solution(mesh):
    return jax.shard_map(
        per_device,
        mesh=mesh,
        in_specs=(
            P("comp", "tile", None, None),
            P("comp", "tile", None, None, None, None),
            P("comp", "tile", None, None),
            P("comp", "tile", None, None),
            P("comp", "tile", None, None),
            P("comp", "tile", None, None),
            P("comp", "tile", None, None),
            P("comp", "tile", None),
            P("comp", "tile", None, None),
            P("comp", "tile", None),
        ),
        out_specs=(
            P("comp", "tile", None, None),
            P("comp", "tile", None),
            P("comp", "tile", None, None),
        ),
        check_vma=False,
    )
```

```python
import functools
import math

import jax
import jax.numpy as jnp
from jax import lax
from jax.experimental import pallas as pl
from jax.experimental.pallas import tpu as pltpu
from jax.sharding import PartitionSpec as P

SUB = 8
MIX = 4
LANES = 128
FIELDS = 5
TERMS_FIRST = 6
STATE_FIRST = 4

heat_gain = 0.5
shortwave_gain = 0.5
wind_mixing = 0.15
relax_rate = 0.5
fresh_gain = 0.5


def shape_of(dims, dtype=jnp.float32):
    return jax.ShapeDtypeStruct(dims, dtype)


def over_groups(x, groups, first):
    order = [[(i + first) % groups for i in range(groups)]]
    return lax.all_to_all(
        x, "comp", split_axis=0, concat_axis=0, axis_index_groups=order, tiled=True
    )


def limit(mib):
    return pltpu.CompilerParams(vmem_limit_bytes=mib << 20)


def cost(flops, moved):
    return pl.CostEstimate(flops=flops, bytes_accessed=moved, transcendentals=0)


VMEM = pl.BlockSpec(memory_space=pltpu.VMEM)
SMEM = pl.BlockSpec(memory_space=pltpu.SMEM)
ANY = pl.BlockSpec(memory_space=pl.ANY)


def terms_kernel(
    src_hbm, cnt_hbm, flux_hbm, weight_hbm, out_hbm,
    src_ref, cnt_ref, flux_ref, blocks_ref, term_ref, held_ref, out_ref, sems, out_sems,
):
    groups, slots = weight_hbm.shape[:2]
    first = [
        pltpu.make_async_copy(src_hbm, src_ref, sems.at[groups]),
        pltpu.make_async_copy(cnt_hbm, cnt_ref, sems.at[groups + 1]),
        pltpu.make_async_copy(flux_hbm, flux_ref, sems.at[groups + 2]),
    ]
    copies = [
        pltpu.make_async_copy(weight_hbm.at[d], held_ref.at[d], sems.at[d]) for d in range(groups)
    ]
    results = [
        pltpu.make_async_copy(out_ref.at[d], out_hbm.at[(d - TERMS_FIRST) % groups], out_sems.at[d])
        for d in range(groups)
    ]
    for copy in first + copies:
        copy.start()
    for copy in first:
        copy.wait()
    for b in range(blocks_ref.shape[0]):
        blocks_ref[b] = flux_ref[:, b * LANES : (b + 1) * LANES].astype(jnp.float32)
    lane = lax.broadcasted_iota(jnp.int32, (8, LANES), 1)
    zero = jnp.zeros((8, LANES), jnp.float32)
    rest = out_ref.shape[1] - FIELDS * slots
    for d in range(groups):
        if d % 2 == 0:
            for copy in copies[d : d + 2]:
                copy.wait()
        for k in range(0, slots, 2):
            parts = []
            for i in (0, 1):
                block = blocks_ref[src_ref[0, 0, d, k + i]]
                parts.append(jnp.where(lane < cnt_ref[0, 0, d, k + i], block, zero))
            top = jnp.concatenate([parts[0], zero], axis=1)
            low = jnp.concatenate([zero, parts[1]], axis=1)
            lhs = jnp.concatenate([top, low], axis=0).astype(jnp.bfloat16)
            rhs = held_ref[d, k : k + 2].reshape(2 * LANES, LANES)
            term_ref[d, k * 8 : k * 8 + 16, :] = jnp.dot(
                lhs, rhs, preferred_element_type=jnp.float32
            )
        f = [term_ref[d, pl.ds(i, slots, stride=8), :] for i in range(8)]
        for i, x in enumerate((f[1], f[0] + f[7], f[2], f[3], f[5] - f[4] + f[6])):
            out_ref[d, i * slots : (i + 1) * slots] = x
        if rest:
            out_ref[d, FIELDS * slots :] = jnp.zeros((rest, LANES), jnp.float32)
        if d % 2 == 1 or d == groups - 1:
            for result in results[d - d % 2 : d + 1]:
                result.start()
    for result in results:
        result.wait()


def remap_terms(src, cnt, flux, weights):
    groups, slots = weights.shape[:2]
    rows = -(-FIELDS * slots // 8) * 8
    return pl.pallas_call(
        terms_kernel,
        in_specs=[ANY] * 4,
        out_specs=ANY,
        out_shape=shape_of((groups, rows, LANES)),
        scratch_shapes=[
            pltpu.SMEM(src.shape, jnp.int32),
            pltpu.SMEM(cnt.shape, jnp.int32),
            pltpu.VMEM(flux.shape, flux.dtype),
            pltpu.VMEM((flux.shape[1] // LANES, 8, LANES), jnp.float32),
            pltpu.VMEM((groups, slots * 8 + 8, LANES), jnp.float32),
            pltpu.VMEM(weights.shape, weights.dtype),
            pltpu.VMEM((groups, rows, LANES), jnp.float32),
            pltpu.SemaphoreType.DMA((groups + 3,)),
            pltpu.SemaphoreType.DMA((groups,)),
        ],
    )(src, cnt, flux, weights)


def target_kernel(after_ref, dst_ref, out_ref, *, rows):
    groups, slots = dst_ref.shape
    dst = dst_ref[...]
    parts = [dst + 8 * f for f in range(FIELDS)]
    rest = rows - FIELDS * slots
    if rest:
        parts.append(jnp.full((groups, rest), -1, jnp.int32))
    ids = jnp.concatenate(parts, axis=1)
    in_order = [(i + TERMS_FIRST) % groups for i in range(groups)]
    line = jnp.concatenate([ids[c : c + 1, :] for c in in_order], axis=1)
    targets = lax.broadcasted_iota(jnp.int32, out_ref.shape, 0)
    hit = jnp.broadcast_to(line, out_ref.shape) == targets
    out_ref[...] = hit.astype(jnp.float32).astype(jnp.bfloat16)


def one_hot_targets(after, dst):
    groups, rows, _ = after.shape
    return pl.pallas_call(
        functools.partial(target_kernel, rows=rows),
        in_specs=[ANY, VMEM],
        out_specs=VMEM,
        out_shape=shape_of((48, groups * rows), jnp.bfloat16),
        cost_estimate=cost(1 << 20, 1 << 20),
        compiler_params=limit(4),
    )(after, dst)


def forcing_kernel(place_ref, arrived_ref, onehot_ref, ssh_ref, off_ref, forcing_ref, pay0_ref, pay1_ref, pay2_ref):
    onehot = onehot_ref[...]
    rest = arrived_ref[...].reshape(-1, LANES)
    total = None
    for _ in range(3):
        piece = rest.astype(jnp.bfloat16)
        part = jnp.dot(onehot, piece, preferred_element_type=jnp.float32)
        total = part if total is None else total + part
        rest = rest - piece.astype(jnp.float32)
    forcing_ref[...] = total[: FIELDS * 8]
    odd = place_ref[0] % 2 == 1
    pieces = [ssh_ref[...], total[(FIELDS - 1) * 8 : FIELDS * 8]]
    pieces += [off_ref[j].astype(jnp.float32) for j in range(off_ref.shape[0])]
    for i, x in enumerate(pieces):
        pay0_ref[4 * i : 4 * i + 4, :] = jnp.where(odd, x[0:4], x[4:8])
        pay1_ref[4 * i : 4 * i + 4, :] = jnp.where(odd, x[4:8], x[0:4])
        pay2_ref[4 * i : 4 * i + 4, :] = jnp.where(odd, x[0:4], x[4:8])


def forcing_and_halo(place, arrived, onehot, ssh, offsets):
    pay = shape_of((4 * (2 + offsets.shape[0]), LANES))
    return pl.pallas_call(
        forcing_kernel,
        in_specs=[SMEM] + [VMEM] * 4,
        out_specs=[VMEM] * 4,
        out_shape=[shape_of((FIELDS * 8, LANES)), pay, pay, pay],
        compiler_params=limit(4),
    )(place, arrived, onehot, ssh, offsets)


def column_parts(forcing_ref):
    east, north = forcing_ref[16:24, :], forcing_ref[24:32, :]
    mixing = wind_mixing * jnp.tanh(jnp.sqrt(east * east + north * north))
    return shortwave_gain * forcing_ref[0:8, :], heat_gain * forcing_ref[8:16, :], mixing


def mix_levels(kappa_ref, forcing_ref, tile_ref, levels):
    short, top, mixing = column_parts(forcing_ref)
    heated, keff = [], []
    for level in range(levels):
        shallow = math.exp(-level / 4.0) - math.exp(-(level + 1.0) / 4.0)
        value = tile_ref[level * 8 : level * 8 + 8, :] + short * shallow
        heated.append(value + top if level == 0 else value)
        if level < levels - 1:
            keff.append(kappa_ref[level] + mixing * math.exp(-level / 4.0))
    for _ in range(MIX):
        above = None
        for level in range(levels):
            here = heated[level]
            if level < levels - 1:
                below = keff[level] * (heated[level + 1] - here)
                new = here + below
            else:
                new = here
            heated[level] = new if above is None else new - above
            above = below
    return heated


def permuted(x, row, col):
    out = jnp.zeros((8, LANES), jnp.float32)
    for s in range(8):
        out = jnp.where(row == s, pick(jnp.broadcast_to(x[s : s + 1, :], (8, LANES)), col), out)
    return out


def pick(x, idx):
    return jnp.take_along_axis(x, idx, axis=1, mode="promise_in_bounds")


def surface_kernel(temp_ref, kappa_ref, forcing_ref, perm_ref, out_ref, tile_ref):
    for b in range(8):
        tile_ref[pl.ds(b, 8, stride=8), :] = temp_ref[:, b * LANES : (b + 1) * LANES]
    heated = mix_levels(kappa_ref, forcing_ref, tile_ref, MIX + 3)
    perm = perm_ref[...]
    row, col = perm >> 7, perm & (LANES - 1)
    for f in (0, 1):
        out_ref[f] = permuted(heated[f], row, col)


def surface_rows(temp, kappa, forcing, perm):
    return pl.pallas_call(
        surface_kernel,
        grid=(1,),
        in_specs=[
            pl.BlockSpec((8, temp.shape[1]), lambda i: (0, 0)),
            pl.BlockSpec((8, 8, LANES), lambda i: (0, 0, 0)),
            pl.BlockSpec(forcing.shape, lambda i: (0, 0)),
            pl.BlockSpec(perm.shape, lambda i: (0, 0)),
        ],
        out_specs=pl.BlockSpec((2, 8, LANES), lambda i: (0, 0, 0)),
        out_shape=shape_of((2, 8, LANES)),
        scratch_shapes=[pltpu.VMEM((72, LANES), jnp.float32)],
        cost_estimate=cost(1 << 20, 1 << 20),
        compiler_params=limit(4),
    )(temp, kappa, forcing, perm)


def column_kernel(height_ref, temp_ref, kappa_ref, forcing_ref, mixed_ref, ssh_out, tile_ref):
    ssh_out[...] = height_ref[...]
    levels = temp_ref.shape[0]
    for b in range(8):
        tile_ref[pl.ds(b, levels, stride=8), :] = temp_ref[:, b * LANES : (b + 1) * LANES]
    heated = mix_levels(kappa_ref, forcing_ref, tile_ref, levels)
    for level in range(levels):
        tile_ref[level * 8 : level * 8 + 8, :] = heated[level]
    for b in range(8):
        mixed_ref[:, b * LANES : (b + 1) * LANES] = tile_ref[pl.ds(b, levels, stride=8), :]


def column_update(height, temp, kappa, forcing):
    return pl.pallas_call(
        column_kernel,
        in_specs=[VMEM] * 4,
        out_specs=[VMEM] * 2,
        out_shape=[shape_of(temp.shape), shape_of(height.shape)],
        scratch_shapes=[pltpu.VMEM((temp.shape[0] * 8 + 8, LANES), jnp.float32)],
        cost_estimate=cost(1 << 22, 1 << 22),
        compiler_params=limit(4),
    )(height, temp, kappa, forcing)


def height_kernel(place_ref, got0_ref, got1_ref, got2_ref, ssh_ref, forcing_ref, off_ref, top_ref, perm_ref, ssh_out, state_out):
    odd, late = place_ref[0] % 2 == 1, place_ref[0] >= 2
    count = off_ref.shape[0]

    def extended(i, own):
        rows = slice(4 * i, 4 * i + 4)
        a, b = jnp.where(late, got2_ref[rows, :], got0_ref[rows, :]), got1_ref[rows, :]
        left, right = jnp.where(odd, a, b), jnp.where(odd, b, a)
        return jnp.concatenate([left, own, right], axis=0)

    eta = extended(0, ssh_ref[...])
    fresh = (fresh_gain / SUB) * extended(1, forcing_ref[(FIELDS - 1) * 8 :, :])
    lane = lax.broadcasted_iota(jnp.int32, (16, LANES), 1)
    places, crossing = [], []
    for j in range(count):
        target = lane + extended(2 + j, off_ref[j].astype(jnp.float32)).astype(jnp.int32)
        places.append(target & (LANES - 1))
        crossing.append((target < 0) | (target >= LANES))
    upper = lane >= LANES // 2
    for _ in range(SUB):
        kept = (1.0 - relax_rate) * eta + fresh
        beside = jnp.where(upper, pltpu.roll(eta, 1, 0), pltpu.roll(eta, 15, 0))
        halves = []
        for h in (0, 8):
            here, other = eta[h : h + 8], beside[h : h + 8]
            near = []
            for j in range(count):
                idx = places[j][h : h + 8]
                near.append(jnp.where(crossing[j][h : h + 8], pick(other, idx), pick(here, idx)))
            while len(near) > 1:
                near = [sum(near[i : i + 2]) for i in range(0, len(near), 2)]
            halves.append(near[0])
        eta = kept + (relax_rate / count) * jnp.concatenate(halves, axis=0)
    height = eta[4:12]
    ssh_out[...] = height
    perm = perm_ref[...]
    out = permuted(height, perm >> 7, perm & (LANES - 1))
    for f, x in enumerate((top_ref[0], top_ref[1], out)):
        for d in range(8):
            state_out[(d - STATE_FIRST) % 8, f : f + 1, :] = x[d : d + 1]


def heights_and_state(place, got0, got1, got2, ssh, forcing, offs, top, perm):
    return pl.pallas_call(
        height_kernel,
        in_specs=[SMEM] + [VMEM] * 8,
        out_specs=[VMEM] * 2,
        out_shape=[pltpu.VMEM((8, LANES), jnp.float32), pltpu.VMEM((8, 3, LANES), jnp.float32)],
        compiler_params=limit(4),
    )(place, got0, got1, got2, ssh, forcing, offs, top, perm)


def per_device(
    atm_flux,
    intersection_weight,
    src_block,
    dst_block,
    intersection_count,
    temp,
    kappa,
    ssh,
    nbr_offset,
    coupler_perm,
):
    tiles, groups = lax.axis_size("tile"), lax.axis_size("comp")
    tile = lax.axis_index("tile")
    place = (tile % 2 + 2 * (tile % 24 >= 22)).astype(jnp.int32).reshape(1)
    height = ssh.reshape(8, LANES)
    perm = coupler_perm.reshape(8, LANES)
    temp, conduct = temp[0, 0], kappa.reshape(kappa.shape[2], 8, LANES)
    offsets = nbr_offset.reshape(nbr_offset.shape[2], 8, LANES)
    terms = remap_terms(src_block, intersection_count, atm_flux[0, 0], intersection_weight[0, 0])
    arrived = over_groups(terms, groups, TERMS_FIRST)
    onehot = one_hot_targets(terms, dst_block[0, 0])
    forcing, pay0, pay1, pay2 = forcing_and_halo(place, arrived, onehot, height, offsets)
    late = [i for i in range(tiles) if i % 24 >= 22]
    inner = [(i, i ^ 1) for i in range(tiles) if i not in late]
    inner_late = [(i, i ^ 1) for i in late]
    outer = [(i, (i - 1 if i % 2 == 0 else i + 1) % tiles) for i in range(tiles)]
    got0 = lax.ppermute(pay0, "tile", inner)
    got1 = lax.ppermute(pay1, "tile", outer)
    got2 = lax.ppermute(pay2, "tile", inner_late)
    top = surface_rows(temp, conduct, forcing, perm)
    height, state = heights_and_state(place, got0, got1, got2, height, forcing, offsets, top, perm)
    mixed, height = column_update(height, temp, conduct, forcing)
    relaid = over_groups(state, groups, STATE_FIRST)
    relaid = jnp.roll(relaid, STATE_FIRST, axis=0)
    coupler_state = relaid.transpose(1, 0, 2).reshape(1, 1, 3, -1)
    return (mixed[None, None], height.reshape(ssh.shape), coupler_state)


def solution(mesh):
    return jax.shard_map(
        per_device,
        mesh=mesh,
        in_specs=(
            P("comp", "tile", None, None),
            P("comp", "tile", None, None, None, None),
            P("comp", "tile", None, None),
            P("comp", "tile", None, None),
            P("comp", "tile", None, None),
            P("comp", "tile", None, None),
            P("comp", "tile", None, None),
            P("comp", "tile", None),
            P("comp", "tile", None, None),
            P("comp", "tile", None),
        ),
        out_specs=(
            P("comp", "tile", None, None),
            P("comp", "tile", None),
            P("comp", "tile", None, None),
        ),
        check_vma=False,
    )
```

```python
import functools
import math

import jax
import jax.numpy as jnp
from jax import lax
from jax.experimental import pallas as pl
from jax.experimental.pallas import tpu as pltpu
from jax.sharding import PartitionSpec as P

SUB = 8
MIX = 4
LANES = 128
FIELDS = 5
TERMS_FIRST = 6
STATE_FIRST = 5

heat_gain = 0.5
shortwave_gain = 0.5
wind_mixing = 0.15
relax_rate = 0.5
fresh_gain = 0.5


def shape_of(dims, dtype=jnp.float32):
    return jax.ShapeDtypeStruct(dims, dtype)


def over_groups(x, groups, first):
    order = [[(i + first) % groups for i in range(groups)]]
    return lax.all_to_all(
        x, "comp", split_axis=0, concat_axis=0, axis_index_groups=order, tiled=True
    )


def limit(mib):
    return pltpu.CompilerParams(vmem_limit_bytes=mib << 20)


def cost(flops, moved):
    return pl.CostEstimate(flops=flops, bytes_accessed=moved, transcendentals=0)


VMEM = pl.BlockSpec(memory_space=pltpu.VMEM)
SMEM = pl.BlockSpec(memory_space=pltpu.SMEM)
ANY = pl.BlockSpec(memory_space=pl.ANY)


def terms_kernel(
    src_hbm, cnt_hbm, flux_hbm, weight_hbm, out_hbm,
    src_ref, cnt_ref, flux_ref, blocks_ref, term_ref, held_ref, out_ref, sems, out_sems,
):
    groups, slots = weight_hbm.shape[:2]
    first = [
        pltpu.make_async_copy(src_hbm, src_ref, sems.at[groups]),
        pltpu.make_async_copy(cnt_hbm, cnt_ref, sems.at[groups + 1]),
        pltpu.make_async_copy(flux_hbm, flux_ref, sems.at[groups + 2]),
    ]
    copies = [
        pltpu.make_async_copy(weight_hbm.at[d], held_ref.at[d], sems.at[d]) for d in range(groups)
    ]
    results = [
        pltpu.make_async_copy(out_ref.at[d], out_hbm.at[(d - TERMS_FIRST) % groups], out_sems.at[d])
        for d in range(groups)
    ]
    for copy in first + copies:
        copy.start()
    for copy in first:
        copy.wait()
    for b in range(blocks_ref.shape[0]):
        blocks_ref[b] = flux_ref[:, b * LANES : (b + 1) * LANES].astype(jnp.float32)
    lane = lax.broadcasted_iota(jnp.int32, (8, LANES), 1)
    zero = jnp.zeros((8, LANES), jnp.float32)
    rest = out_ref.shape[1] - FIELDS * slots
    for d in range(groups):
        if d % 2 == 0:
            for copy in copies[d : d + 2]:
                copy.wait()
        for k in range(0, slots, 2):
            parts = []
            for i in (0, 1):
                block = blocks_ref[src_ref[0, 0, d, k + i]]
                parts.append(jnp.where(lane < cnt_ref[0, 0, d, k + i], block, zero))
            top = jnp.concatenate([parts[0], zero], axis=1)
            low = jnp.concatenate([zero, parts[1]], axis=1)
            lhs = jnp.concatenate([top, low], axis=0).astype(jnp.bfloat16)
            rhs = held_ref[d, k : k + 2].reshape(2 * LANES, LANES)
            term_ref[d, k * 8 : k * 8 + 16, :] = jnp.dot(
                lhs, rhs, preferred_element_type=jnp.float32
            )
        f = [term_ref[d, pl.ds(i, slots, stride=8), :] for i in range(8)]
        for i, x in enumerate((f[1], f[0] + f[7], f[2], f[3], f[5] - f[4] + f[6])):
            out_ref[d, i * slots : (i + 1) * slots] = x
        if rest:
            out_ref[d, FIELDS * slots :] = jnp.zeros((rest, LANES), jnp.float32)
        if d % 2 == 1 or d == groups - 1:
            for result in results[d - d % 2 : d + 1]:
                result.start()
    for result in results:
        result.wait()


def remap_terms(src, cnt, flux, weights):
    groups, slots = weights.shape[:2]
    rows = -(-FIELDS * slots // 8) * 8
    return pl.pallas_call(
        terms_kernel,
        in_specs=[ANY] * 4,
        out_specs=ANY,
        out_shape=shape_of((groups, rows, LANES)),
        scratch_shapes=[
            pltpu.SMEM(src.shape, jnp.int32),
            pltpu.SMEM(cnt.shape, jnp.int32),
            pltpu.VMEM(flux.shape, flux.dtype),
            pltpu.VMEM((flux.shape[1] // LANES, 8, LANES), jnp.float32),
            pltpu.VMEM((groups, slots * 8 + 8, LANES), jnp.float32),
            pltpu.VMEM(weights.shape, weights.dtype),
            pltpu.VMEM((groups, rows, LANES), jnp.float32),
            pltpu.SemaphoreType.DMA((groups + 3,)),
            pltpu.SemaphoreType.DMA((groups,)),
        ],
    )(src, cnt, flux, weights)


def target_kernel(after_ref, dst_ref, out_ref, *, rows):
    groups, slots = dst_ref.shape
    dst = dst_ref[...]
    parts = [dst + 8 * f for f in range(FIELDS)]
    rest = rows - FIELDS * slots
    if rest:
        parts.append(jnp.full((groups, rest), -1, jnp.int32))
    ids = jnp.concatenate(parts, axis=1)
    in_order = [(i + TERMS_FIRST) % groups for i in range(groups)]
    line = jnp.concatenate([ids[c : c + 1, :] for c in in_order], axis=1)
    targets = lax.broadcasted_iota(jnp.int32, out_ref.shape, 0)
    hit = jnp.broadcast_to(line, out_ref.shape) == targets
    out_ref[...] = hit.astype(jnp.float32).astype(jnp.bfloat16)


def one_hot_targets(after, dst):
    groups, rows, _ = after.shape
    return pl.pallas_call(
        functools.partial(target_kernel, rows=rows),
        in_specs=[ANY, VMEM],
        out_specs=VMEM,
        out_shape=shape_of((48, groups * rows), jnp.bfloat16),
        cost_estimate=cost(1 << 20, 1 << 20),
        compiler_params=limit(4),
    )(after, dst)


def forcing_kernel(place_ref, arrived_ref, onehot_ref, ssh_ref, off_ref, forcing_ref, pay0_ref, pay1_ref, pay2_ref):
    onehot = onehot_ref[...]
    rest = arrived_ref[...].reshape(-1, LANES)
    total = None
    for _ in range(3):
        piece = rest.astype(jnp.bfloat16)
        part = jnp.dot(onehot, piece, preferred_element_type=jnp.float32)
        total = part if total is None else total + part
        rest = rest - piece.astype(jnp.float32)
    forcing_ref[...] = total[: FIELDS * 8]
    odd = place_ref[0] % 2 == 1
    pieces = [ssh_ref[...], total[(FIELDS - 1) * 8 : FIELDS * 8]]
    pieces += [off_ref[j].astype(jnp.float32) for j in range(off_ref.shape[0])]
    for i, x in enumerate(pieces):
        pay0_ref[4 * i : 4 * i + 4, :] = jnp.where(odd, x[0:4], x[4:8])
        pay1_ref[4 * i : 4 * i + 4, :] = jnp.where(odd, x[4:8], x[0:4])
        pay2_ref[4 * i : 4 * i + 4, :] = jnp.where(odd, x[0:4], x[4:8])


def forcing_and_halo(place, arrived, onehot, ssh, offsets):
    pay = shape_of((4 * (2 + offsets.shape[0]), LANES))
    return pl.pallas_call(
        forcing_kernel,
        in_specs=[SMEM] + [VMEM] * 4,
        out_specs=[VMEM] * 4,
        out_shape=[shape_of((FIELDS * 8, LANES)), pay, pay, pay],
        compiler_params=limit(4),
    )(place, arrived, onehot, ssh, offsets)


def column_parts(forcing_ref):
    east, north = forcing_ref[16:24, :], forcing_ref[24:32, :]
    mixing = wind_mixing * jnp.tanh(jnp.sqrt(east * east + north * north))
    return shortwave_gain * forcing_ref[0:8, :], heat_gain * forcing_ref[8:16, :], mixing


def mix_levels(kappa_ref, forcing_ref, tile_ref, levels):
    short, top, mixing = column_parts(forcing_ref)
    heated, keff = [], []
    for level in range(levels):
        shallow = math.exp(-level / 4.0) - math.exp(-(level + 1.0) / 4.0)
        value = tile_ref[level * 8 : level * 8 + 8, :] + short * shallow
        heated.append(value + top if level == 0 else value)
        if level < levels - 1:
            keff.append(kappa_ref[level] + mixing * math.exp(-level / 4.0))
    for _ in range(MIX):
        above = None
        for level in range(levels):
            here = heated[level]
            if level < levels - 1:
                below = keff[level] * (heated[level + 1] - here)
                new = here + below
            else:
                new = here
            heated[level] = new if above is None else new - above
            above = below
    return heated


def permuted(x, row, col):
    out = jnp.zeros((8, LANES), jnp.float32)
    for s in range(8):
        out = jnp.where(row == s, pick(jnp.broadcast_to(x[s : s + 1, :], (8, LANES)), col), out)
    return out


def pick(x, idx):
    return jnp.take_along_axis(x, idx, axis=1, mode="promise_in_bounds")


def surface_kernel(temp_ref, kappa_ref, forcing_ref, perm_ref, out_ref, tile_ref):
    for b in range(8):
        tile_ref[pl.ds(b, 8, stride=8), :] = temp_ref[:, b * LANES : (b + 1) * LANES]
    heated = mix_levels(kappa_ref, forcing_ref, tile_ref, MIX + 3)
    perm = perm_ref[...]
    row, col = perm >> 7, perm & (LANES - 1)
    for f in (0, 1):
        out_ref[f] = permuted(heated[f], row, col)


def surface_rows(temp, kappa, forcing, perm):
    return pl.pallas_call(
        surface_kernel,
        grid=(1,),
        in_specs=[
            pl.BlockSpec((8, temp.shape[1]), lambda i: (0, 0)),
            pl.BlockSpec((8, 8, LANES), lambda i: (0, 0, 0)),
            pl.BlockSpec(forcing.shape, lambda i: (0, 0)),
            pl.BlockSpec(perm.shape, lambda i: (0, 0)),
        ],
        out_specs=pl.BlockSpec((2, 8, LANES), lambda i: (0, 0, 0)),
        out_shape=shape_of((2, 8, LANES)),
        scratch_shapes=[pltpu.VMEM((72, LANES), jnp.float32)],
        cost_estimate=cost(1 << 20, 1 << 20),
        compiler_params=limit(4),
    )(temp, kappa, forcing, perm)


def column_kernel(height_ref, temp_ref, kappa_ref, forcing_ref, mixed_ref, ssh_out, tile_ref):
    ssh_out[...] = height_ref[...]
    levels = temp_ref.shape[0]
    for b in range(8):
        tile_ref[pl.ds(b, levels, stride=8), :] = temp_ref[:, b * LANES : (b + 1) * LANES]
    heated = mix_levels(kappa_ref, forcing_ref, tile_ref, levels)
    for level in range(levels):
        tile_ref[level * 8 : level * 8 + 8, :] = heated[level]
    for b in range(8):
        mixed_ref[:, b * LANES : (b + 1) * LANES] = tile_ref[pl.ds(b, levels, stride=8), :]


def column_update(height, temp, kappa, forcing):
    return pl.pallas_call(
        column_kernel,
        in_specs=[VMEM] * 4,
        out_specs=[VMEM] * 2,
        out_shape=[shape_of(temp.shape), shape_of(height.shape)],
        scratch_shapes=[pltpu.VMEM((temp.shape[0] * 8 + 8, LANES), jnp.float32)],
        cost_estimate=cost(1 << 22, 1 << 22),
        compiler_params=limit(4),
    )(height, temp, kappa, forcing)


def height_kernel(place_ref, got0_ref, got1_ref, got2_ref, ssh_ref, forcing_ref, off_ref, top_ref, perm_ref, ssh_out, state_out):
    odd, late = place_ref[0] % 2 == 1, place_ref[0] >= 2
    count = off_ref.shape[0]

    def extended(i, own):
        rows = slice(4 * i, 4 * i + 4)
        a, b = jnp.where(late, got2_ref[rows, :], got0_ref[rows, :]), got1_ref[rows, :]
        left, right = jnp.where(odd, a, b), jnp.where(odd, b, a)
        return jnp.concatenate([left, own, right], axis=0)

    eta = extended(0, ssh_ref[...])
    fresh = (fresh_gain / SUB) * extended(1, forcing_ref[(FIELDS - 1) * 8 :, :])
    lane = lax.broadcasted_iota(jnp.int32, (16, LANES), 1)
    places, crossing = [], []
    for j in range(count):
        target = lane + extended(2 + j, off_ref[j].astype(jnp.float32)).astype(jnp.int32)
        places.append(target & (LANES - 1))
        crossing.append((target < 0) | (target >= LANES))
    upper = lane >= LANES // 2
    for _ in range(SUB):
        kept = (1.0 - relax_rate) * eta + fresh
        beside = jnp.where(upper, pltpu.roll(eta, 1, 0), pltpu.roll(eta, 15, 0))
        halves = []
        for h in (0, 8):
            here, other = eta[h : h + 8], beside[h : h + 8]
            near = []
            for j in range(count):
                idx = places[j][h : h + 8]
                near.append(jnp.where(crossing[j][h : h + 8], pick(other, idx), pick(here, idx)))
            while len(near) > 1:
                near = [sum(near[i : i + 2]) for i in range(0, len(near), 2)]
            halves.append(near[0])
        eta = kept + (relax_rate / count) * jnp.concatenate(halves, axis=0)
    height = eta[4:12]
    ssh_out[...] = height
    perm = perm_ref[...]
    out = permuted(height, perm >> 7, perm & (LANES - 1))
    for f, x in enumerate((top_ref[0], top_ref[1], out)):
        for d in range(8):
            state_out[(d - STATE_FIRST) % 8, f : f + 1, :] = x[d : d + 1]


def heights_and_state(place, got0, got1, got2, ssh, forcing, offs, top, perm):
    return pl.pallas_call(
        height_kernel,
        in_specs=[SMEM] + [VMEM] * 8,
        out_specs=[VMEM] * 2,
        out_shape=[pltpu.VMEM((8, LANES), jnp.float32), pltpu.VMEM((8, 3, LANES), jnp.float32)],
        compiler_params=limit(4),
    )(place, got0, got1, got2, ssh, forcing, offs, top, perm)


def per_device(
    atm_flux,
    intersection_weight,
    src_block,
    dst_block,
    intersection_count,
    temp,
    kappa,
    ssh,
    nbr_offset,
    coupler_perm,
):
    tiles, groups = lax.axis_size("tile"), lax.axis_size("comp")
    tile = lax.axis_index("tile")
    place = (tile % 2 + 2 * (tile % 24 >= 22)).astype(jnp.int32).reshape(1)
    height = ssh.reshape(8, LANES)
    perm = coupler_perm.reshape(8, LANES)
    temp, conduct = temp[0, 0], kappa.reshape(kappa.shape[2], 8, LANES)
    offsets = nbr_offset.reshape(nbr_offset.shape[2], 8, LANES)
    terms = remap_terms(src_block, intersection_count, atm_flux[0, 0], intersection_weight[0, 0])
    arrived = over_groups(terms, groups, TERMS_FIRST)
    onehot = one_hot_targets(terms, dst_block[0, 0])
    forcing, pay0, pay1, pay2 = forcing_and_halo(place, arrived, onehot, height, offsets)
    late = [i for i in range(tiles) if i % 24 >= 22]
    inner = [(i, i ^ 1) for i in range(tiles) if i not in late]
    inner_late = [(i, i ^ 1) for i in late]
    outer = [(i, (i - 1 if i % 2 == 0 else i + 1) % tiles) for i in range(tiles)]
    got0 = lax.ppermute(pay0, "tile", inner)
    got1 = lax.ppermute(pay1, "tile", outer)
    got2 = lax.ppermute(pay2, "tile", inner_late)
    top = surface_rows(temp, conduct, forcing, perm)
    height, state = heights_and_state(place, got0, got1, got2, height, forcing, offsets, top, perm)
    mixed, height = column_update(height, temp, conduct, forcing)
    relaid = over_groups(state, groups, STATE_FIRST)
    relaid = jnp.roll(relaid, STATE_FIRST, axis=0)
    coupler_state = relaid.transpose(1, 0, 2).reshape(1, 1, 3, -1)
    return (mixed[None, None], height.reshape(ssh.shape), coupler_state)


def solution(mesh):
    return jax.shard_map(
        per_device,
        mesh=mesh,
        in_specs=(
            P("comp", "tile", None, None),
            P("comp", "tile", None, None, None, None),
            P("comp", "tile", None, None),
            P("comp", "tile", None, None),
            P("comp", "tile", None, None),
            P("comp", "tile", None, None),
            P("comp", "tile", None, None),
            P("comp", "tile", None),
            P("comp", "tile", None, None),
            P("comp", "tile", None),
        ),
        out_specs=(
            P("comp", "tile", None, None),
            P("comp", "tile", None),
            P("comp", "tile", None, None),
        ),
        check_vma=False,
    )
```
